512 devices in a mesh: ctx: 128 (over y, z, x_hi), grp: 4 (over x_lo, core).
Axes of the slice: x: 4 (x_hi: 2, x_lo: 2; x = x_hi * 2 + x_lo), y: 4, z: 16, core: 2. Of those that a mesh axis runs over, the one named last changes fastest.
Arguments:
- queries: bfloat16 [2048, 6144], P('ctx'), may hold values from -9 to 9
- keys: bfloat16 [30720, 512], P(('ctx', 'grp')), may hold values from -6 to 6
- values: bfloat16 [30720, 512], P(('ctx', 'grp')), may hold values from -6 to 6
- own_keys: bfloat16 [2048, 512], P('ctx', 'grp'), may hold values from -12 to 12
- own_values: bfloat16 [2048, 512], P('ctx', 'grp'), may hold values from -6 to 6
Outputs:
- attended: bfloat16 [2048, 6144], P('ctx', 'grp')
The draws below stay inside these ranges and needn't reach their ends.
All inputs are finite; a program needn't handle non-finite values.
Results may differ from the reference program's by a relative error of at most 0.0055.
Values may be sent and summed in bfloat16 or wider, within the bound.
A program may use at most 64 MiB of HBM per device.

```python
import jax
import jax.numpy as jnp
from jax import lax

HS = 128
KVH = 4
HQ = 48
QROWS = 2048
CONTEXT = 30720


def draw_queries(key, part):
    key = jax.random.fold_in(key, 1)
    entries = jnp.clip(3.0 * jax.random.normal(key, (QROWS, HQ * HS), jnp.float32), -9.0, 9.0)
    return entries.astype(jnp.bfloat16)


def draw_keys(key, part):
    key = jax.random.fold_in(key, 2)
    entries = jnp.clip(jax.random.normal(key, (CONTEXT, KVH * HS), jnp.float32), -6.0, 6.0)
    return entries.astype(jnp.bfloat16)


def block_levels(key, dims, split, smallest, largest):
    factor_of, own = 1.0, jax.random.fold_in(key, 6)
    for dim, shards_of in split:
        steps = jnp.exp(jax.random.uniform(jax.random.fold_in(own, dim), (shards_of,), jnp.float32, smallest / len(split), largest / len(split)))
        factor_of = factor_of * jnp.repeat(steps, dims[dim] // shards_of).reshape([-1 if axis == dim else 1 for axis in range(len(dims))])
    return factor_of


def noise(rng, dims, spread, limit, cuts=(), kind=jnp.bfloat16):
    result = spread * jax.random.normal(rng, dims, jnp.float32)
    if cuts:
        result = result * block_levels(rng, dims, cuts, -0.22, 0.18)
    return jnp.clip(result, -limit, limit).astype(kind)


def setup_inputs(seed: int = 0) -> dict:
    key_of = jax.random.split(jax.random.key(seed), 6)
    return {
        "queries": draw_queries(jax.random.fold_in(key_of[5], 71), 0),
        "keys": draw_keys(jax.random.fold_in(key_of[5], 71), 0),
        "values": noise(key_of[2], (CONTEXT, KVH * HS), 1.0, 6.0, ((0, 512),)),
        "own_keys": noise(key_of[3], (QROWS, KVH * HS), 3.0, 12.0, ((0, 128), (1, 4))),
        "own_values": noise(key_of[4], (QROWS, KVH * HS), 1.0, 6.0, ((0, 128), (1, 4))),
    }


def reference(queries, keys, values, own_keys, own_values):
    group_size = HQ // KVH
    score_scale = HS ** -0.5
    row_block = min(QROWS, 64)
    block_count = QROWS // row_block
    query_grid = queries.reshape(QROWS, KVH, group_size, HS)
    key_grid = keys.reshape(CONTEXT, KVH, HS)
    value_grid = values.reshape(CONTEXT, KVH, HS)
    own_key_grid = own_keys.reshape(QROWS, KVH, HS)
    own_value_grid = own_values.reshape(QROWS, KVH, HS)

    def per_head(head_index):
        head_keys = lax.dynamic_index_in_dim(key_grid, head_index, 1, False).astype(jnp.float32)
        head_values = lax.dynamic_index_in_dim(value_grid, head_index, 1, False).astype(jnp.float32)
        head_queries = lax.dynamic_index_in_dim(query_grid, head_index, 1, False)
        head_own_keys = lax.dynamic_index_in_dim(own_key_grid, head_index, 1, False)
        head_own_values = lax.dynamic_index_in_dim(own_value_grid, head_index, 1, False)

        def per_block(block_index):
            start = (block_index * row_block).astype(jnp.int32)
            block_queries = lax.dynamic_slice_in_dim(head_queries, start, row_block, 0).astype(jnp.float32)
            block_own_keys = lax.dynamic_slice_in_dim(head_own_keys, start, row_block, 0).astype(jnp.float32)
            block_own_values = lax.dynamic_slice_in_dim(head_own_values, start, row_block, 0).astype(jnp.float32)
            scores = jnp.einsum("rth,ch->trc", block_queries, head_keys) * score_scale
            own_scores = jnp.einsum("rth,rh->tr", block_queries, block_own_keys) * score_scale
            top_score = jnp.maximum(jnp.max(scores, axis=-1), own_scores)
            weights = jnp.exp(scores - top_score[..., None])
            own_weights = jnp.exp(own_scores - top_score)
            totals = jnp.sum(weights, axis=-1) + own_weights
            rounded = lax.optimization_barrier(weights.astype(jnp.bfloat16)).astype(jnp.float32)
            own_rounded = lax.optimization_barrier(own_weights.astype(jnp.bfloat16)).astype(jnp.float32)
            mixed = jnp.einsum("trc,ch->trh", rounded, head_values)
            mixed = mixed + own_rounded[..., None] * block_own_values[None]
            return mixed / totals[..., None]

        return lax.map(per_block, jnp.arange(block_count, dtype=jnp.int32))

    outcome = lax.map(per_head, jnp.arange(KVH, dtype=jnp.int32))
    outcome = outcome.transpose(1, 3, 0, 2, 4).reshape(QROWS, HQ * HS)
    return outcome.astype(jnp.bfloat16)
```

```python
import functools
import math

import jax
import jax.numpy as jnp
from jax import lax
from jax.experimental import pallas as pl
from jax.experimental.pallas import tpu as pltpu
from jax.sharding import PartitionSpec as P

MESH = pl.DeviceIdType.MESH
HS = 128
KVH = 4
GROUP = 12
ROWS = 16
XS, YS, ZS = 4, 4, 16
KEYS = 60
PAD = 64
HALF = ZS // 2
SLOTS = ZS
SCALE = math.log2(math.e) / math.sqrt(HS)
QB = GROUP * ROWS
LANES = 16


def device(x, y, z, c):
    return {"ctx": (y * ZS + z) * 2 + x // 2, "grp": lax.rem(x, 2) * 2 + c}


def head_of(x):
    return x // 2 + 2 * (1 - lax.rem(x, 2))


def nt(a, b):
    return lax.dot_general(a, b, (((1,), (1,)), ((), ())), preferred_element_type=jnp.float32)


def kernel(
    q_ref, k_ref, v_ref, ok_ref, ov_ref, out_ref,
    pad32, kvst, qs, qbuf, kv, sib, acc, top, own, omsg, orecv,
    first_send, ring_send, ring_recv, sib_send, sib_recv, q_send, q_recv, o_send, o_recv,
):
    ctx, grp = lax.axis_index("ctx"), lax.axis_index("grp")
    xhi, z, y = lax.rem(ctx, 2), lax.rem(ctx // 2, ZS), ctx // (2 * ZS)
    xlo, c = grp // 2, lax.rem(grp, 2)
    x = 2 * xhi + xlo
    mine = head_of(x)

    def at_x(dx):
        return lax.rem(x + dx, XS)

    def at_y(dy):
        return lax.rem(y + dy, YS)

    z_next = (lax.rem(z + 1, ZS), lax.rem(z + ZS - 1, ZS), z)
    sibling = device(x, y, z, 1 - c)
    q_x = jnp.where(c == 0, x, XS - 1 - x)
    q_self = jnp.logical_and(c == 0, xhi == 0)
    q_from_own = c == xhi
    q_from_x = jnp.where(q_from_own, x, XS - 1 - x)
    q_from_c = jnp.where(q_from_own, 0, 1)
    o_x, o_c = 2 * c + mine // 2, lax.rem(mine, 2)
    o_from_x, o_from_c = 2 * c + 1 - xlo, xhi

    barrier = pltpu.get_barrier_semaphore()

    def greet(to):
        pl.semaphore_signal(barrier, inc=1, device_id=to, device_id_type=MESH)

    for dz in (0, 1):
        for dx in range(XS):
            greet(device(at_x(dx), y, z_next[dz], c))
    for dx in range(1, XS):
        greet(device(at_x(dx), y, z, c))
    greet(sibling)
    for dy in range(YS):
        greet(device(o_from_x, at_y(dy), z, o_from_c))
        if dy:
            greet(device(q_from_x, at_y(dy), z, q_from_c))

    @pl.when(jnp.logical_not(q_self))
    def _():
        greet(device(q_from_x, y, z, q_from_c))

    for which, ref in ((0, k_ref), (1, v_ref)):
        rows = ref[...].astype(jnp.float32)
        pad32[0:KEYS, :] = rows
        if which == 0:
            pad32[KEYS:PAD, :] = rows[0 : PAD - KEYS, :]
        else:
            pad32[KEYS:PAD, :] = jnp.zeros((PAD - KEYS, KVH * HS), jnp.float32)
        for h in range(KVH):
            kvst[h, which] = pad32[:, h * HS : (h + 1) * HS].astype(jnp.bfloat16)
    for h in range(KVH * GROUP):
        qs[h] = q_ref[:, h * HS : (h + 1) * HS]

    expected = 2 * XS + XS - 1 + 1 + 2 * YS - 1
    pl.semaphore_wait(barrier, jnp.where(q_self, expected, expected + 1))

    def first(dz, dx):
        to = at_x(dx)
        slot = (1, 2, 0)[dz]
        return pltpu.make_async_remote_copy(
            src_ref=kvst.at[head_of(to)],
            dst_ref=kv.at[slot, x],
            send_sem=first_send.at[dz, dx],
            recv_sem=ring_recv.at[slot, x],
            device_id=device(to, y, z_next[dz], c),
            device_id_type=MESH,
        )

    def query(dy):
        return pltpu.make_async_remote_copy(
            src_ref=qs.at[pl.ds(head_of(q_x) * GROUP, GROUP)],
            dst_ref=qbuf.at[(YS - dy) % YS],
            send_sem=q_send.at[dy],
            recv_sem=q_recv.at[(YS - dy) % YS],
            device_id=device(q_x, at_y(dy), z, xhi),
            device_id_type=MESH,
        )

    for dx in (2, 1, 3, 0):
        for dz in (0, 1):
            first(dz, dx).start()
    for dx in (2, 1, 3):
        first(2, dx).start()
    for dy in (2, 1, 3):
        query(dy).start()

    @pl.when(jnp.logical_not(q_self))
    def _():
        query(0).start()

    @pl.when(q_self)
    def _():
        qbuf[0] = qs[pl.ds(mine * GROUP, GROUP)]

    kv[0, x] = kvst[mine]

    def forward(d, slot, to_slot, piece):
        return pltpu.make_async_remote_copy(
            src_ref=kv.at[slot, piece],
            dst_ref=kv.at[to_slot, piece],
            send_sem=ring_send.at[slot, piece],
            recv_sem=ring_recv.at[to_slot, piece],
            device_id=device(x, y, z_next[d], c),
            device_id_type=MESH,
        )

    def arrived(d, slot, piece):
        forward(d, slot, slot, piece).wait_recv()

    def across(slot):
        return pltpu.make_async_remote_copy(
            src_ref=kv.at[slot],
            dst_ref=sib.at[slot],
            send_sem=sib_send.at[slot],
            recv_sem=sib_recv.at[slot],
            device_id=sibling,
            device_id_type=MESH,
        )

    lane = lax.broadcasted_iota(jnp.int32, (ROWS, HS), 1)
    own_scores = jnp.zeros((ROWS, HS), jnp.float32)
    group = 2 * xlo + c
    own_key = ok_ref[...].astype(jnp.float32)
    for h in range(GROUP):
        product = qs[group * GROUP + h].astype(jnp.float32) * own_key
        score = jnp.sum(product, axis=1, keepdims=True) * SCALE
        own_scores = jnp.where(lane == h, score, own_scores)
    own[...] = own_scores

    top[...] = jnp.full(top.shape, -1e30, jnp.float32)
    acc[...] = jnp.zeros(acc.shape, jnp.float32)
    real = lax.broadcasted_iota(jnp.int32, (8, PAD, HS), 1) < KEYS
    ones = jnp.where(real, 1.0, 0.0).astype(jnp.bfloat16).reshape(8 * PAD, HS)

    def block_of(slot):
        keys = jnp.concatenate(
            [kv[slot, :, 0].reshape(4 * PAD, HS), sib[slot, :, 0].reshape(4 * PAD, HS)], axis=0
        )
        values = jnp.concatenate(
            [kv[slot, :, 1].reshape(4 * PAD, HS), sib[slot, :, 1].reshape(4 * PAD, HS)], axis=0
        )
        return keys, jnp.concatenate([values, ones], axis=1)

    def absorb(i, keys, values):
        scores = nt(qbuf[i].reshape(QB, HS), keys) * SCALE
        before = top[i][:, :1]
        best = jnp.max(scores, axis=1, keepdims=True).astype(jnp.bfloat16).astype(jnp.float32)
        now = jnp.maximum(before, best)
        weights = jnp.exp2(scores - now).astype(jnp.bfloat16)
        mixed = jnp.dot(weights, values, preferred_element_type=jnp.float32)
        acc[i] = acc[i] * jnp.exp2(before - now) + mixed
        top[i] = jnp.broadcast_to(now, (QB, HS))

    def compute(slot):
        across(slot).wait_recv()
        keys, values = block_of(slot)

        def turn(i, _):
            absorb(i, keys, values)
            return 0

        lax.fori_loop(0, YS, turn, 0)

    for dx in (1, 2, 3):
        arrived(0, 0, at_x(dx))
    across(0).start()
    for dy in (1, 2, 3):
        query(dy).wait_recv()

    @pl.when(jnp.logical_not(q_self))
    def _():
        query(0).wait_recv()

    def step(s, _):
        slot = 2 * s - 1
        for piece in range(XS):
            for d in (0, 1):
                arrived(d, slot + d, piece)
                forward(d, slot + d, slot + 2 + d, piece).start()
        for d in (0, 1):
            across(slot + d).start()
        compute(slot - 1)
        compute(slot)
        return 0

    lax.fori_loop(1, HALF - 1, step, 0)
    slot = 2 * HALF - 3
    for piece in range(XS):
        for d in (0, 1):
            arrived(d, slot + d, piece)
            if piece // 2 == d:
                forward(d, slot + d, SLOTS - 1, piece).start()
    for d in (0, 1):
        across(slot + d).start()
    compute(slot - 1)
    compute(slot)
    for piece in range(XS):
        arrived(piece // 2, SLOTS - 1, piece)
    across(SLOTS - 1).start()
    compute(SLOTS - 2)

    def result(dy):
        return pltpu.make_async_remote_copy(
            src_ref=omsg.at[dy],
            dst_ref=orecv.at[(YS - dy) % YS],
            send_sem=o_send.at[dy],
            recv_sem=o_recv.at[(YS - dy) % YS],
            device_id=device(o_x, at_y(dy), z, o_c),
            device_id_type=MESH,
        )

    across(SLOTS - 1).wait_recv()
    keys, values = block_of(SLOTS - 1)
    for dy in (2, 1, 3, 0):
        absorb(dy, keys, values)
        omsg[dy, 0:GROUP] = acc[dy, :, :HS].astype(jnp.bfloat16).reshape(GROUP, ROWS, HS)
        stats = jnp.zeros((ROWS, HS), jnp.float32)
        for h in range(GROUP):
            rows = slice(h * ROWS, (h + 1) * ROWS)
            total = acc[dy, rows, HS:]
            high = total.astype(jnp.bfloat16).astype(jnp.float32)
            stats = jnp.where(lane == h, top[dy, rows], stats)
            stats = jnp.where(lane == LANES + h, high, stats)
            stats = jnp.where(lane == 2 * LANES + h, total - high, stats)
        omsg[dy, GROUP] = stats.astype(jnp.bfloat16)
        result(dy).start()

    for dy in range(YS):
        result(dy).wait_recv()
    largest = own[...]
    tops, totals = [], []
    for i in range(YS):
        stats = orecv[i, GROUP].astype(jnp.float32)
        tops.append(stats)
        totals.append(pltpu.roll(stats, HS - LANES, 1) + pltpu.roll(stats, HS - 2 * LANES, 1))
        largest = jnp.maximum(largest, stats)
    own_factor = jnp.exp2(own[...] - largest)
    factors = [jnp.exp2(t - largest) for t in tops]
    total = own_factor
    for factor, part in zip(factors, totals):
        total = total + factor * part
    own_factor = own_factor / total
    factors = [factor / total for factor in factors]
    own_value = ov_ref[...].astype(jnp.float32)
    for h in range(GROUP):
        mixed = own_factor[:, h : h + 1] * own_value
        for i in range(YS):
            mixed = mixed + factors[i][:, h : h + 1] * orecv[i, h].astype(jnp.float32)
        out_ref[:, h * HS : (h + 1) * HS] = mixed.astype(jnp.bfloat16)

    for dz in range(3):
        for dx in range(XS):
            if dz < 2 or dx:
                first(dz, dx).wait_send()
    for dy in (1, 2, 3):
        query(dy).wait_send()

    @pl.when(jnp.logical_not(q_self))
    def _():
        query(0).wait_send()

    def sent(slot, _):
        for piece in range(XS):
            forward(0, slot, slot, piece).wait_send()
        return 0

    lax.fori_loop(1, SLOTS - 3, sent, 0)
    for piece in range(XS):
        forward(0, slot + piece // 2, SLOTS - 1, piece).wait_send()

    def crossed(slot, _):
        across(slot).wait_send()
        return 0

    lax.fori_loop(0, SLOTS, crossed, 0)
    for dy in range(YS):
        result(dy).wait_send()


def local(queries, keys, values, own_keys, own_values):
    vmem = pl.BlockSpec(memory_space=pltpu.VMEM)
    bf16, f32 = jnp.bfloat16, jnp.float32
    dma = pltpu.SemaphoreType.DMA
    return pl.pallas_call(
        kernel,
        out_shape=jax.ShapeDtypeStruct((ROWS, GROUP * HS), bf16),
        in_specs=[vmem] * 5,
        out_specs=vmem,
        scratch_shapes=[
            pltpu.VMEM((PAD, KVH * HS), f32),
            pltpu.VMEM((KVH, 2, PAD, HS), bf16),
            pltpu.VMEM((KVH * GROUP, ROWS, HS), bf16),
            pltpu.VMEM((YS, GROUP, ROWS, HS), bf16),
            pltpu.VMEM((SLOTS, XS, 2, PAD, HS), bf16),
            pltpu.VMEM((SLOTS, XS, 2, PAD, HS), bf16),
            pltpu.VMEM((YS, QB, 2 * HS), f32),
            pltpu.VMEM((YS, QB, HS), f32),
            pltpu.VMEM((ROWS, HS), f32),
            pltpu.VMEM((YS, GROUP + 1, ROWS, HS), bf16),
            pltpu.VMEM((YS, GROUP + 1, ROWS, HS), bf16),
            dma((3, XS)),
            dma((SLOTS, XS)),
            dma((SLOTS, XS)),
            dma((SLOTS,)),
            dma((SLOTS,)),
            dma((YS,)),
            dma((YS,)),
            dma((YS,)),
            dma((YS,)),
        ],
        compiler_params=pltpu.CompilerParams(
            collective_id=0, has_side_effects=True, vmem_limit_bytes=40 << 20
        ),
    )(queries, keys, values, own_keys, own_values)


def solution(mesh):
    placed = (
        P("ctx", None),
        P(("ctx", "grp"), None),
        P(("ctx", "grp"), None),
        P("ctx", "grp"),
        P("ctx", "grp"),
    )
    return jax.shard_map(
        local, mesh=mesh, in_specs=placed, out_specs=P("ctx", "grp"), check_vma=False
    )
```

```python
import functools
import math

import jax
import jax.numpy as jnp
from jax import lax
from jax.experimental import pallas as pl
from jax.experimental.pallas import tpu as pltpu
from jax.sharding import PartitionSpec as P

MESH = pl.DeviceIdType.MESH
HS = 128
KVH = 4
GROUP = 12
ROWS = 16
XS, YS, ZS = 4, 4, 16
KEYS = 60
PAD = 64
HALF = ZS // 2
SLOTS = ZS
SCALE = math.log2(math.e) / math.sqrt(HS)
QB = GROUP * ROWS
LANES = 16


def device(x, y, z, c):
    return {"ctx": (y * ZS + z) * 2 + x // 2, "grp": lax.rem(x, 2) * 2 + c}


def head_of(x):
    return x // 2 + 2 * (1 - lax.rem(x, 2))


def nt(a, b):
    return lax.dot_general(a, b, (((1,), (1,)), ((), ())), preferred_element_type=jnp.float32)


def kernel(
    q_hbm, k_hbm, v_hbm, ok_hbm, ov_hbm, out_ref,
    q_ref, k_ref, v_ref, ok_ref, ov_ref, in_sem, pad32, kvst, qs, qbuf, kv, sib, acc, top, own, omsg, orecv,
    first_send, ring_send, ring_recv, sib_send, sib_recv, q_send, q_recv, o_send, o_recv,
):
    fetches = [
        pltpu.make_async_copy(source, to, in_sem.at[i])
        for i, (source, to) in enumerate(
            ((k_hbm, k_ref), (v_hbm, v_ref), (q_hbm, q_ref), (ok_hbm, ok_ref), (ov_hbm, ov_ref))
        )
    ]
    for fetch in fetches:
        fetch.start()
    ctx, grp = lax.axis_index("ctx"), lax.axis_index("grp")
    xhi, z, y = lax.rem(ctx, 2), lax.rem(ctx // 2, ZS), ctx // (2 * ZS)
    xlo, c = grp // 2, lax.rem(grp, 2)
    x = 2 * xhi + xlo
    mine = head_of(x)

    def at_x(dx):
        return lax.rem(x + dx, XS)

    def at_y(dy):
        return lax.rem(y + dy, YS)

    z_next = (lax.rem(z + 1, ZS), lax.rem(z + ZS - 1, ZS), z)
    sibling = device(x, y, z, 1 - c)
    q_x = jnp.where(c == 0, x, XS - 1 - x)
    q_self = jnp.logical_and(c == 0, xhi == 0)
    q_from_own = c == xhi
    q_from_x = jnp.where(q_from_own, x, XS - 1 - x)
    q_from_c = jnp.where(q_from_own, 0, 1)
    o_x, o_c = 2 * c + mine // 2, lax.rem(mine, 2)
    o_from_x, o_from_c = 2 * c + 1 - xlo, xhi

    barrier = pltpu.get_barrier_semaphore()

    def greet(to):
        pl.semaphore_signal(barrier, inc=1, device_id=to, device_id_type=MESH)

    for dz in (0, 1):
        for dx in range(XS):
            greet(device(at_x(dx), y, z_next[dz], c))
    for dx in range(1, XS):
        greet(device(at_x(dx), y, z, c))
    greet(sibling)
    for dy in range(YS):
        greet(device(o_from_x, at_y(dy), z, o_from_c))
        if dy:
            greet(device(q_from_x, at_y(dy), z, q_from_c))

    @pl.when(jnp.logical_not(q_self))
    def _():
        greet(device(q_from_x, y, z, q_from_c))

    for which, ref in ((0, k_ref), (1, v_ref)):
        fetches[which].wait()
        rows = ref[...].astype(jnp.float32)
        pad32[0:KEYS, :] = rows
        if which == 0:
            pad32[KEYS:PAD, :] = rows[0 : PAD - KEYS, :]
        else:
            pad32[KEYS:PAD, :] = jnp.zeros((PAD - KEYS, KVH * HS), jnp.float32)
        for h in range(KVH):
            kvst[h, which] = pad32[:, h * HS : (h + 1) * HS].astype(jnp.bfloat16)
    expected = 2 * XS + XS - 1 + 1 + 2 * YS - 1
    pl.semaphore_wait(barrier, jnp.where(q_self, expected, expected + 1))

    def first(dz, dx):
        to = at_x(dx)
        slot = (1, 2, 0)[dz]
        return pltpu.make_async_remote_copy(
            src_ref=kvst.at[head_of(to)],
            dst_ref=kv.at[slot, x],
            send_sem=first_send.at[dz, dx],
            recv_sem=ring_recv.at[slot, x],
            device_id=device(to, y, z_next[dz], c),
            device_id_type=MESH,
        )

    def query(dy):
        return pltpu.make_async_remote_copy(
            src_ref=qs.at[pl.ds(head_of(q_x) * GROUP, GROUP)],
            dst_ref=qbuf.at[(YS - dy) % YS],
            send_sem=q_send.at[dy],
            recv_sem=q_recv.at[(YS - dy) % YS],
            device_id=device(q_x, at_y(dy), z, xhi),
            device_id_type=MESH,
        )

    for dx in (2, 1, 3, 0):
        for dz in (0, 1):
            first(dz, dx).start()
    for dx in (2, 1, 3):
        first(2, dx).start()
    kv[0, x] = kvst[mine]
    fetches[2].wait()
    for h in range(KVH * GROUP):
        qs[h] = q_ref[:, h * HS : (h + 1) * HS]
    for dy in (2, 1, 3):
        query(dy).start()

    @pl.when(jnp.logical_not(q_self))
    def _():
        query(0).start()

    @pl.when(q_self)
    def _():
        qbuf[0] = qs[pl.ds(mine * GROUP, GROUP)]

    def forward(d, slot, to_slot, piece):
        return pltpu.make_async_remote_copy(
            src_ref=kv.at[slot, piece],
            dst_ref=kv.at[to_slot, piece],
            send_sem=ring_send.at[slot, piece],
            recv_sem=ring_recv.at[to_slot, piece],
            device_id=device(x, y, z_next[d], c),
            device_id_type=MESH,
        )

    def arrived(d, slot, piece):
        forward(d, slot, slot, piece).wait_recv()

    def across(slot):
        return pltpu.make_async_remote_copy(
            src_ref=kv.at[slot],
            dst_ref=sib.at[slot],
            send_sem=sib_send.at[slot],
            recv_sem=sib_recv.at[slot],
            device_id=sibling,
            device_id_type=MESH,
        )

    fetches[3].wait()
    fetches[4].wait()

    lane = lax.broadcasted_iota(jnp.int32, (ROWS, HS), 1)
    own_scores = jnp.zeros((ROWS, HS), jnp.float32)
    group = 2 * xlo + c
    own_key = ok_ref[...].astype(jnp.float32)
    for h in range(GROUP):
        product = qs[group * GROUP + h].astype(jnp.float32) * own_key
        score = jnp.sum(product, axis=1, keepdims=True)
        own_scores = jnp.where(lane == h, score, own_scores)
    own[...] = own_scores

    top[...] = jnp.full(top.shape, -1e30, jnp.float32)
    acc[...] = jnp.zeros(acc.shape, jnp.float32)
    real = lax.broadcasted_iota(jnp.int32, (8, PAD, HS), 1) < KEYS
    ones = jnp.where(real, 1.0, 0.0).astype(jnp.bfloat16).reshape(8 * PAD, HS)

    def block_of(slot):
        keys = [held[slot, :, 0].reshape(4 * PAD, HS) for held in (kv, sib)]
        values = [held[slot, :, 1].reshape(4 * PAD, HS) for held in (kv, sib)]
        values = jnp.concatenate(values, axis=0)
        return jnp.concatenate(keys, axis=0), jnp.concatenate([values, ones], axis=1)

    def absorb(i, keys, values):
        scores = nt(qbuf[i].reshape(QB, HS), keys)
        before = top[i]
        best = jnp.max(scores, axis=1, keepdims=True).astype(jnp.bfloat16).astype(jnp.float32)
        now = jnp.maximum(before, jnp.broadcast_to(best, (QB, HS)))
        top[i] = now
        scaled = now * SCALE
        weights = [
            jnp.exp2(scores[:, k : k + HS] * SCALE - scaled).astype(jnp.bfloat16)
            for k in range(0, keys.shape[0], HS)
        ]
        mixed = jnp.dot(
            jnp.concatenate(weights, axis=1), values, preferred_element_type=jnp.float32
        )
        factor = jnp.exp2((before - now) * SCALE)
        acc[i] = acc[i] * jnp.concatenate([factor, factor], axis=1) + mixed

    def compute(*slots):
        for slot in slots:
            across(slot).wait_recv()
        blocks = [block_of(slot) for slot in slots]
        keys = jnp.concatenate([block[0] for block in blocks], axis=0)
        values = jnp.concatenate([block[1] for block in blocks], axis=0)
        for i in range(YS):
            absorb(i, keys, values)

    for dx in (1, 2, 3):
        arrived(0, 0, at_x(dx))
    across(0).start()
    for dy in (1, 2, 3):
        query(dy).wait_recv()

    @pl.when(jnp.logical_not(q_self))
    def _():
        query(0).wait_recv()

    def pass_on(s):
        slot = 2 * s - 1
        for piece in range(XS):
            for d in (0, 1):
                arrived(d, slot + d, piece)
                to_slot = jnp.minimum(slot + 2 + d, SLOTS - 1)

                @pl.when(jnp.logical_or(s < HALF - 1, piece // 2 == d))
                def _():
                    forward(d, slot + d, to_slot, piece).start()

        for d in (0, 1):
            across(slot + d).start()

    pass_on(jnp.int32(1))
    compute(0)

    def step(s, _):
        pass_on(s)
        compute(2 * s - 3, 2 * s - 2)
        return 0

    lax.fori_loop(2, HALF, step, 0)
    compute(SLOTS - 3, SLOTS - 2)
    for piece in range(XS):
        arrived(piece // 2, SLOTS - 1, piece)
    across(SLOTS - 1).start()

    def result(dy):
        return pltpu.make_async_remote_copy(
            src_ref=omsg.at[dy],
            dst_ref=orecv.at[(YS - dy) % YS],
            send_sem=o_send.at[dy],
            recv_sem=o_recv.at[(YS - dy) % YS],
            device_id=device(o_x, at_y(dy), z, o_c),
            device_id_type=MESH,
        )

    across(SLOTS - 1).wait_recv()
    keys, values = block_of(SLOTS - 1)
    for dy in (2, 1, 3, 0):
        absorb(dy, keys, values)
        omsg[dy, 0:GROUP] = acc[dy, :, :HS].astype(jnp.bfloat16).reshape(GROUP, ROWS, HS)
        stats = jnp.zeros((ROWS, HS), jnp.float32)
        for h in range(GROUP):
            rows = slice(h * ROWS, (h + 1) * ROWS)
            total = acc[dy, rows, HS:]
            high = total.astype(jnp.bfloat16).astype(jnp.float32)
            stats = jnp.where(lane == h, top[dy, rows], stats)
            stats = jnp.where(lane == LANES + h, high, stats)
            stats = jnp.where(lane == 2 * LANES + h, total - high, stats)
        omsg[dy, GROUP] = stats.astype(jnp.bfloat16)
        result(dy).start()

    for dz in range(3):
        for dx in range(XS):
            if dz < 2 or dx:
                first(dz, dx).wait_send()
    for dy in (1, 2, 3):
        query(dy).wait_send()

    @pl.when(jnp.logical_not(q_self))
    def _():
        query(0).wait_send()

    def sent(slot, _):
        for piece in range(XS):
            forward(0, slot, slot, piece).wait_send()
        return 0

    lax.fori_loop(1, SLOTS - 3, sent, 0)
    for piece in range(XS):
        forward(0, SLOTS - 3 + piece // 2, SLOTS - 1, piece).wait_send()

    def crossed(slot, _):
        across(slot).wait_send()
        return 0

    lax.fori_loop(0, SLOTS, crossed, 0)

    for dy in range(YS):
        result(dy).wait_recv()
    largest = own[...]
    tops, totals = [], []
    for i in range(YS):
        stats = orecv[i, GROUP].astype(jnp.float32)
        tops.append(stats)
        totals.append(pltpu.roll(stats, HS - LANES, 1) + pltpu.roll(stats, HS - 2 * LANES, 1))
        largest = jnp.maximum(largest, stats)
    own_factor = jnp.exp2((own[...] - largest) * SCALE)
    factors = [jnp.exp2((t - largest) * SCALE) for t in tops]
    total = own_factor
    for factor, part in zip(factors, totals):
        total = total + factor * part
    own_factor = own_factor / total
    factors = [factor / total for factor in factors]
    own_value = ov_ref[...].astype(jnp.float32)
    for h in range(GROUP):
        mixed = own_factor[:, h : h + 1] * own_value
        for i in range(YS):
            mixed = mixed + factors[i][:, h : h + 1] * orecv[i, h].astype(jnp.float32)
        out_ref[:, h * HS : (h + 1) * HS] = mixed.astype(jnp.bfloat16)
    for dy in range(YS):
        result(dy).wait_send()


def local(queries, keys, values, own_keys, own_values):
    vmem = pl.BlockSpec(memory_space=pltpu.VMEM)
    bf16, f32 = jnp.bfloat16, jnp.float32
    dma = pltpu.SemaphoreType.DMA
    return pl.pallas_call(
        kernel,
        out_shape=jax.ShapeDtypeStruct((ROWS, GROUP * HS), bf16),
        in_specs=[pl.BlockSpec(memory_space=pl.ANY)] * 5,
        out_specs=vmem,
        scratch_shapes=[
            pltpu.VMEM((ROWS, KVH * GROUP * HS), bf16),
            pltpu.VMEM((KEYS, KVH * HS), bf16),
            pltpu.VMEM((KEYS, KVH * HS), bf16),
            pltpu.VMEM((ROWS, HS), bf16),
            pltpu.VMEM((ROWS, HS), bf16),
            dma((5,)),
            pltpu.VMEM((PAD, KVH * HS), f32),
            pltpu.VMEM((KVH, 2, PAD, HS), bf16),
            pltpu.VMEM((KVH * GROUP, ROWS, HS), bf16),
            pltpu.VMEM((YS, GROUP, ROWS, HS), bf16),
            pltpu.VMEM((SLOTS, XS, 2, PAD, HS), bf16),
            pltpu.VMEM((SLOTS, XS, 2, PAD, HS), bf16),
            pltpu.VMEM((YS, QB, 2 * HS), f32),
            pltpu.VMEM((YS, QB, HS), f32),
            pltpu.VMEM((ROWS, HS), f32),
            pltpu.VMEM((YS, GROUP + 1, ROWS, HS), bf16),
            pltpu.VMEM((YS, GROUP + 1, ROWS, HS), bf16),
            dma((3, XS)),
            dma((SLOTS, XS)),
            dma((SLOTS, XS)),
            dma((SLOTS,)),
            dma((SLOTS,)),
            dma((YS,)),
            dma((YS,)),
            dma((YS,)),
            dma((YS,)),
        ],
        compiler_params=pltpu.CompilerParams(
            collective_id=0, has_side_effects=True, vmem_limit_bytes=60 << 20
        ),
    )(queries, keys, values, own_keys, own_values)


def solution(mesh):
    placed = (
        P("ctx", None),
        P(("ctx", "grp"), None),
        P(("ctx", "grp"), None),
        P("ctx", "grp"),
        P("ctx", "grp"),
    )
    return jax.shard_map(
        local, mesh=mesh, in_specs=placed, out_specs=P("ctx", "grp"), check_vma=False
    )
```

```python
import functools
import math

import jax
import jax.numpy as jnp
from jax import lax
from jax.experimental import pallas as pl
from jax.experimental.pallas import tpu as pltpu
from jax.sharding import PartitionSpec as P

MESH = pl.DeviceIdType.MESH
HS = 128
KVH = 4
GROUP = 12
ROWS = 16
XS, YS, ZS = 4, 4, 16
KEYS = 60
PAD = 64
HALF = ZS // 2
SLOTS = ZS
SCALE = math.log2(math.e) / math.sqrt(HS)
QB = GROUP * ROWS
LANES = 16


def device(x, y, z, c):
    return {"ctx": (y * ZS + z) * 2 + x // 2, "grp": lax.rem(x, 2) * 2 + c}


def head_of(x):
    return x // 2 + 2 * (1 - lax.rem(x, 2))


def nt(a, b):
    return lax.dot_general(a, b, (((1,), (1,)), ((), ())), preferred_element_type=jnp.float32)


def kernel(
    q_hbm, k_hbm, v_hbm, ok_hbm, ov_hbm, out_ref,
    q_ref, k_ref, v_ref, ok_ref, ov_ref, in_sem, pad32, kvst, qs, qbuf, kv, sib, acc, top, own, omsg, orecv,
    first_send, ring_send, ring_recv, sib_send, sib_recv, q_send, q_recv, o_send, o_recv,
):
    fetches = [
        pltpu.make_async_copy(source, to, in_sem.at[i])
        for i, (source, to) in enumerate(
            ((k_hbm, k_ref), (v_hbm, v_ref), (q_hbm, q_ref), (ok_hbm, ok_ref), (ov_hbm, ov_ref))
        )
    ]
    for fetch in fetches:
        fetch.start()
    ctx, grp = lax.axis_index("ctx"), lax.axis_index("grp")
    xhi, z, y = lax.rem(ctx, 2), lax.rem(ctx // 2, ZS), ctx // (2 * ZS)
    xlo, c = grp // 2, lax.rem(grp, 2)
    x = 2 * xhi + xlo
    mine = head_of(x)

    def at_x(dx):
        return lax.rem(x + dx, XS)

    def at_y(dy):
        return lax.rem(y + dy, YS)

    z_next = (lax.rem(z + 1, ZS), lax.rem(z + ZS - 1, ZS), z)
    sibling = device(x, y, z, 1 - c)
    q_self = c == xhi
    q_x = jnp.where(q_self, x, XS - 1 - x)
    o_x, o_c = 2 * c + mine // 2, lax.rem(mine, 2)

    barrier = pltpu.get_barrier_semaphore()

    def greet(to):
        pl.semaphore_signal(barrier, inc=1, device_id=to, device_id_type=MESH)

    for dz in (0, 1):
        for dx in (1, 3, 0):
            greet(device(at_x(dx), y, z_next[dz], c))
    for dx in range(1, XS):
        greet(device(at_x(dx), y, z, c))
    greet(sibling)
    for dy in range(1, YS):
        greet(device(q_x, at_y(dy), z, xhi))

    @pl.when(jnp.logical_not(q_self))
    def _():
        greet(device(q_x, y, z, xhi))

    for which, ref in ((0, k_ref), (1, v_ref)):
        fetches[which].wait()
        rows = ref[...].astype(jnp.float32)
        pad32[0:KEYS, :] = rows
        if which == 0:
            pad32[KEYS:PAD, :] = rows[0 : PAD - KEYS, :]
        else:
            pad32[KEYS:PAD, :] = jnp.zeros((PAD - KEYS, KVH * HS), jnp.float32)
        for h in range(KVH):
            kvst[h, which] = pad32[:, h * HS : (h + 1) * HS].astype(jnp.bfloat16)
    expected = 2 * (XS - 1) + XS - 1 + 1 + YS - 1
    pl.semaphore_wait(barrier, jnp.where(q_self, expected, expected + 1))

    def first(dz, dx):
        to = at_x(dx)
        slot = (1, 2, 0)[dz]
        return pltpu.make_async_remote_copy(
            src_ref=kvst.at[head_of(to)],
            dst_ref=kv.at[slot, x],
            send_sem=first_send.at[dz, dx],
            recv_sem=ring_recv.at[slot, x],
            device_id=device(to, y, z_next[dz], c),
            device_id_type=MESH,
        )

    def query(dy):
        return pltpu.make_async_remote_copy(
            src_ref=qs.at[pl.ds(head_of(q_x) * GROUP, GROUP)],
            dst_ref=qbuf.at[(YS - dy) % YS],
            send_sem=q_send.at[dy],
            recv_sem=q_recv.at[(YS - dy) % YS],
            device_id=device(q_x, at_y(dy), z, xhi),
            device_id_type=MESH,
        )

    first(2, 2).start()
    for dx in (1, 3, 0):
        for dz in (0, 1):
            first(dz, dx).start()
    for dx in (1, 3):
        first(2, dx).start()
    kv[0, x] = kvst[mine]
    fetches[2].wait()
    for h in range(KVH * GROUP):
        qs[h] = q_ref[:, h * HS : (h + 1) * HS]
    for dy in (2, 1, 3):
        query(dy).start()

    @pl.when(jnp.logical_not(q_self))
    def _():
        query(0).start()

    @pl.when(q_self)
    def _():
        qbuf[0] = qs[pl.ds(mine * GROUP, GROUP)]

    def forward(d, slot, to_slot, piece):
        return pltpu.make_async_remote_copy(
            src_ref=kv.at[slot, piece],
            dst_ref=kv.at[to_slot, piece],
            send_sem=ring_send.at[slot, piece],
            recv_sem=ring_recv.at[to_slot, piece],
            device_id=device(x, y, z_next[d], c),
            device_id_type=MESH,
        )

    def arrived(d, slot, piece):
        forward(d, slot, slot, piece).wait_recv()

    def across(slot):
        return pltpu.make_async_remote_copy(
            src_ref=kv.at[slot],
            dst_ref=sib.at[slot],
            send_sem=sib_send.at[slot],
            recv_sem=sib_recv.at[slot],
            device_id=sibling,
            device_id_type=MESH,
        )

    fetches[3].wait()
    fetches[4].wait()

    lane = lax.broadcasted_iota(jnp.int32, (ROWS, HS), 1)
    own_scores = jnp.zeros((ROWS, HS), jnp.float32)
    group = 2 * xlo + c
    own_key = ok_ref[...].astype(jnp.float32)
    for h in range(GROUP):
        product = qs[group * GROUP + h].astype(jnp.float32) * own_key
        score = jnp.sum(product, axis=1, keepdims=True)
        own_scores = jnp.where(lane == h, score, own_scores)
    own[...] = own_scores

    top[...] = jnp.full(top.shape, -1e30, jnp.float32)
    acc[...] = jnp.zeros(acc.shape, jnp.float32)
    real = lax.broadcasted_iota(jnp.int32, (8, PAD, HS), 1) < KEYS
    ones = jnp.where(real, 1.0, 0.0).astype(jnp.bfloat16).reshape(8 * PAD, HS)

    def block_of(slot):
        keys = [held[slot, :, 0].reshape(4 * PAD, HS) for held in (kv, sib)]
        values = [held[slot, :, 1].reshape(4 * PAD, HS) for held in (kv, sib)]
        values = jnp.concatenate(values, axis=0)
        return jnp.concatenate(keys, axis=0), jnp.concatenate([values, ones], axis=1)

    def absorb(i, keys, values):
        scores = nt(qbuf[i].reshape(QB, HS), keys)
        before = top[i]
        best = jnp.max(scores, axis=1, keepdims=True).astype(jnp.bfloat16).astype(jnp.float32)
        now = jnp.maximum(before, jnp.broadcast_to(best, (QB, HS)))
        top[i] = now
        scaled = now * SCALE
        weights = [
            jnp.exp2(scores[:, k : k + HS] * SCALE - scaled).astype(jnp.bfloat16)
            for k in range(0, keys.shape[0], HS)
        ]
        mixed = jnp.dot(
            jnp.concatenate(weights, axis=1), values, preferred_element_type=jnp.float32
        )
        factor = jnp.exp2((before - now) * SCALE)
        acc[i] = acc[i] * jnp.concatenate([factor, factor], axis=1) + mixed

    def compute(*slots):
        for slot in slots:
            across(slot).wait_recv()
        blocks = [block_of(slot) for slot in slots]
        keys = jnp.concatenate([block[0] for block in blocks], axis=0)
        values = jnp.concatenate([block[1] for block in blocks], axis=0)
        for i in range(YS):
            absorb(i, keys, values)

    def relay(d):
        return pltpu.make_async_remote_copy(
            src_ref=kv.at[0, at_x(2)],
            dst_ref=kv.at[1 + d, at_x(2)],
            send_sem=first_send.at[d, 2],
            recv_sem=ring_recv.at[1 + d, at_x(2)],
            device_id=device(x, y, z_next[d], c),
            device_id_type=MESH,
        )

    arrived(0, 0, at_x(2))
    for d in (0, 1):
        relay(d).start()
    for dx in (1, 3):
        arrived(0, 0, at_x(dx))
    across(0).start()
    for dy in (1, 2, 3):
        query(dy).wait_recv()

    @pl.when(jnp.logical_not(q_self))
    def _():
        query(0).wait_recv()

    pieces = [(at_x(0), 0), (at_x(1), 0), (at_x(3), 1), (at_x(2), 1)]

    def pass_on(s):
        slot = 2 * s - 1
        for piece, side in pieces:
            for d in (0, 1):
                arrived(d, slot + d, piece)
                to_slot = jnp.minimum(slot + 2 + d, SLOTS - 1)

                @pl.when(jnp.logical_or(s < HALF - 1, side == d))
                def _():
                    forward(d, slot + d, to_slot, piece).start()

        for d in (0, 1):
            across(slot + d).start()

    pass_on(jnp.int32(1))
    compute(0)

    def step(s, _):
        pass_on(s)
        compute(2 * s - 3, 2 * s - 2)
        return 0

    lax.fori_loop(2, HALF, step, 0)
    compute(SLOTS - 3, SLOTS - 2)
    for piece, side in pieces:
        arrived(side, SLOTS - 1, piece)
    across(SLOTS - 1).start()

    def result(dy):
        return pltpu.make_async_remote_copy(
            src_ref=omsg.at[dy],
            dst_ref=orecv.at[(YS - dy) % YS],
            send_sem=o_send.at[dy],
            recv_sem=o_recv.at[(YS - dy) % YS],
            device_id=device(o_x, at_y(dy), z, o_c),
            device_id_type=MESH,
        )

    across(SLOTS - 1).wait_recv()
    keys, values = block_of(SLOTS - 1)
    for dy in (2, 1, 3, 0):
        absorb(dy, keys, values)
        omsg[dy, 0:GROUP] = acc[dy, :, :HS].astype(jnp.bfloat16).reshape(GROUP, ROWS, HS)
        stats = jnp.zeros((ROWS, HS), jnp.float32)
        for h in range(GROUP):
            rows = slice(h * ROWS, (h + 1) * ROWS)
            total = acc[dy, rows, HS:]
            high = total.astype(jnp.bfloat16).astype(jnp.float32)
            stats = jnp.where(lane == h, top[dy, rows], stats)
            stats = jnp.where(lane == LANES + h, high, stats)
            stats = jnp.where(lane == 2 * LANES + h, total - high, stats)
        omsg[dy, GROUP] = stats.astype(jnp.bfloat16)
        result(dy).start()

    for dz in range(3):
        for dx in range(XS):
            if dz < 2 or dx:
                first(dz, dx).wait_send()
    for dy in (1, 2, 3):
        query(dy).wait_send()

    @pl.when(jnp.logical_not(q_self))
    def _():
        query(0).wait_send()

    def sent(slot, _):
        for piece in range(XS):
            forward(0, slot, slot, piece).wait_send()
        return 0

    lax.fori_loop(1, SLOTS - 3, sent, 0)
    for piece, side in pieces:
        forward(0, SLOTS - 3 + side, SLOTS - 1, piece).wait_send()

    def crossed(slot, _):
        across(slot).wait_send()
        return 0

    lax.fori_loop(0, SLOTS, crossed, 0)

    for dy in range(YS):
        result(dy).wait_recv()
    largest = own[...]
    tops, totals = [], []
    for i in range(YS):
        stats = orecv[i, GROUP].astype(jnp.float32)
        tops.append(stats)
        totals.append(pltpu.roll(stats, HS - LANES, 1) + pltpu.roll(stats, HS - 2 * LANES, 1))
        largest = jnp.maximum(largest, stats)
    own_factor = jnp.exp2((own[...] - largest) * SCALE)
    factors = [jnp.exp2((t - largest) * SCALE) for t in tops]
    total = own_factor
    for factor, part in zip(factors, totals):
        total = total + factor * part
    own_factor = own_factor / total
    factors = [factor / total for factor in factors]
    own_value = ov_ref[...].astype(jnp.float32)
    for h in range(GROUP):
        mixed = own_factor[:, h : h + 1] * own_value
        for i in range(YS):
            mixed = mixed + factors[i][:, h : h + 1] * orecv[i, h].astype(jnp.float32)
        out_ref[:, h * HS : (h + 1) * HS] = mixed.astype(jnp.bfloat16)
    for dy in range(YS):
        result(dy).wait_send()


def local(queries, keys, values, own_keys, own_values):
    vmem = pl.BlockSpec(memory_space=pltpu.VMEM)
    bf16, f32 = jnp.bfloat16, jnp.float32
    dma = pltpu.SemaphoreType.DMA
    return pl.pallas_call(
        kernel,
        out_shape=jax.ShapeDtypeStruct((ROWS, GROUP * HS), bf16),
        in_specs=[pl.BlockSpec(memory_space=pl.ANY)] * 5,
        out_specs=vmem,
        scratch_shapes=[
            pltpu.VMEM((ROWS, KVH * GROUP * HS), bf16),
            pltpu.VMEM((KEYS, KVH * HS), bf16),
            pltpu.VMEM((KEYS, KVH * HS), bf16),
            pltpu.VMEM((ROWS, HS), bf16),
            pltpu.VMEM((ROWS, HS), bf16),
            dma((5,)),
            pltpu.VMEM((PAD, KVH * HS), f32),
            pltpu.VMEM((KVH, 2, PAD, HS), bf16),
            pltpu.VMEM((KVH * GROUP, ROWS, HS), bf16),
            pltpu.VMEM((YS, GROUP, ROWS, HS), bf16),
            pltpu.VMEM((SLOTS, XS, 2, PAD, HS), bf16),
            pltpu.VMEM((SLOTS, XS, 2, PAD, HS), bf16),
            pltpu.VMEM((YS, QB, 2 * HS), f32),
            pltpu.VMEM((YS, QB, HS), f32),
            pltpu.VMEM((ROWS, HS), f32),
            pltpu.VMEM((YS, GROUP + 1, ROWS, HS), bf16),
            pltpu.VMEM((YS, GROUP + 1, ROWS, HS), bf16),
            dma((3, XS)),
            dma((SLOTS, XS)),
            dma((SLOTS, XS)),
            dma((SLOTS,)),
            dma((SLOTS,)),
            dma((YS,)),
            dma((YS,)),
            dma((YS,)),
            dma((YS,)),
        ],
        compiler_params=pltpu.CompilerParams(
            collective_id=0, has_side_effects=True, vmem_limit_bytes=60 << 20
        ),
    )(queries, keys, values, own_keys, own_values)


def solution(mesh):
    placed = (
        P("ctx", None),
        P(("ctx", "grp"), None),
        P(("ctx", "grp"), None),
        P("ctx", "grp"),
        P("ctx", "grp"),
    )
    return jax.shard_map(
        local, mesh=mesh, in_specs=placed, out_specs=P("ctx", "grp"), check_vma=False
    )
```

```python
import functools
import math

import jax
import jax.numpy as jnp
from jax import lax
from jax.experimental import pallas as pl
from jax.experimental.pallas import tpu as pltpu
from jax.sharding import PartitionSpec as P

MESH = pl.DeviceIdType.MESH
HS = 128
KVH = 4
GROUP = 12
ROWS = 16
XS, YS, ZS = 4, 4, 16
KEYS = 60
PAD = 64
HALF = ZS // 2
PIECES = 2 * XS
PLACE = (0, 1, 3, 2)
SCALE = math.log2(math.e) / math.sqrt(HS)
QB = GROUP * ROWS
LANES = 16


def device(x, y, z, c):
    return {"ctx": (y * ZS + z) * 2 + x // 2, "grp": lax.rem(x, 2) * 2 + c}


def head_of(x):
    return x // 2 + 2 * (1 - lax.rem(x, 2))


def nt(a, b):
    return lax.dot_general(a, b, (((1,), (1,)), ((), ())), preferred_element_type=jnp.float32)


def kernel(
    q_hbm, k_hbm, v_hbm, ok_hbm, ov_hbm, out_ref,
    q_ref, k_ref, v_ref, ok_ref, ov_ref, in_sem, pad32, kvst, qs, qbuf, near, kv, sib, far, acc, top, own, omsg, orecv,
    first_send, relay_send, ring_send, ring_recv, last_send, last_recv, sib_send, sib_recv,
    near_recv, q_send, q_recv, o_send, o_recv,
):
    fetches = [
        pltpu.make_async_copy(source, to, in_sem.at[i])
        for i, (source, to) in enumerate(
            ((k_hbm, k_ref), (v_hbm, v_ref), (q_hbm, q_ref), (ok_hbm, ok_ref), (ov_hbm, ov_ref))
        )
    ]
    for fetch in fetches:
        fetch.start()
    ctx, grp = lax.axis_index("ctx"), lax.axis_index("grp")
    xhi, z, y = lax.rem(ctx, 2), lax.rem(ctx // 2, ZS), ctx // (2 * ZS)
    xlo, c = grp // 2, lax.rem(grp, 2)
    x = 2 * xhi + xlo
    mine = head_of(x)

    def at_x(dx):
        return lax.rem(x + dx, XS)

    def at_y(dy):
        return lax.rem(y + dy, YS)

    z_up, z_down = lax.rem(z + 1, ZS), lax.rem(z + ZS - 1, ZS)
    z_to = jnp.where(c == 0, z_up, z_down)
    z_from = jnp.where(c == 0, z_down, z_up)
    sibling = device(x, y, z, 1 - c)
    q_self = c == xhi
    q_x = jnp.where(q_self, x, XS - 1 - x)
    o_x, o_c = 2 * c + mine // 2, lax.rem(mine, 2)

    barrier = pltpu.get_barrier_semaphore()

    def greet(to):
        pl.semaphore_signal(barrier, inc=1, device_id=to, device_id_type=MESH)

    for dx in (1, 3, 0):
        for core in (0, 1):
            greet(device(at_x(dx), y, z_from, core))
    greet(device(x, y, z_to, 1 - c))
    for dx in range(1, XS):
        greet(device(at_x(dx), y, z, c))
    greet(sibling)
    for dy in range(1, YS):
        greet(device(q_x, at_y(dy), z, xhi))

    @pl.when(jnp.logical_not(q_self))
    def _():
        greet(device(q_x, y, z, xhi))

    for which, ref in ((0, k_ref), (1, v_ref)):
        fetches[which].wait()
        rows = ref[...].astype(jnp.float32)
        pad32[0:KEYS, :] = rows
        if which == 0:
            pad32[KEYS:PAD, :] = rows[0 : PAD - KEYS, :]
        else:
            pad32[KEYS:PAD, :] = jnp.zeros((PAD - KEYS, KVH * HS), jnp.float32)
        for h in range(KVH):
            kvst[h, which] = pad32[:, h * HS : (h + 1) * HS].astype(jnp.bfloat16)
    expected = 2 * (XS - 1) + 1 + XS - 1 + 1 + YS - 1
    pl.semaphore_wait(barrier, jnp.where(q_self, expected, expected + 1))

    def here(dx):
        to = at_x(dx)
        return pltpu.make_async_remote_copy(
            src_ref=kvst.at[head_of(to)],
            dst_ref=near.at[PLACE[(XS - dx) % XS]],
            send_sem=first_send.at[2, dx],
            recv_sem=near_recv.at[PLACE[(XS - dx) % XS]],
            device_id=device(to, y, z, c),
            device_id_type=MESH,
        )

    def first(way, dx):
        to = at_x(dx)
        return pltpu.make_async_remote_copy(
            src_ref=kvst.at[head_of(to)],
            dst_ref=kv.at[0, 2 * PLACE[(XS - dx) % XS] + c],
            send_sem=first_send.at[way, dx],
            recv_sem=ring_recv.at[0, 2 * PLACE[(XS - dx) % XS] + c],
            device_id=device(to, y, (z_up, z_down)[way], way),
            device_id_type=MESH,
        )

    def query(dy):
        return pltpu.make_async_remote_copy(
            src_ref=qs.at[pl.ds(head_of(q_x) * GROUP, GROUP)],
            dst_ref=qbuf.at[(YS - dy) % YS],
            send_sem=q_send.at[dy],
            recv_sem=q_recv.at[(YS - dy) % YS],
            device_id=device(q_x, at_y(dy), z, xhi),
            device_id_type=MESH,
        )

    here(2).start()
    for dx in (1, 3, 0):
        for way in (0, 1):
            first(way, dx).start()
    for dx in (1, 3):
        here(dx).start()
    near[0] = kvst[mine]
    fetches[2].wait()
    for h in range(KVH * GROUP):
        qs[h] = q_ref[:, h * HS : (h + 1) * HS]
    for dy in (2, 1, 3):
        query(dy).start()

    @pl.when(jnp.logical_not(q_self))
    def _():
        query(0).start()

    @pl.when(q_self)
    def _():
        qbuf[0] = qs[pl.ds(mine * GROUP, GROUP)]

    def forward(step, piece):
        return pltpu.make_async_remote_copy(
            src_ref=kv.at[step, piece],
            dst_ref=kv.at[step + 1, piece],
            send_sem=ring_send.at[step, piece],
            recv_sem=ring_recv.at[step + 1, piece],
            device_id=device(x, y, z_to, c),
            device_id_type=MESH,
        )

    def arrived(step, piece):
        pltpu.make_async_remote_copy(
            src_ref=kv.at[step, piece],
            dst_ref=kv.at[step, piece],
            send_sem=ring_send.at[step, piece],
            recv_sem=ring_recv.at[step, piece],
            device_id=device(x, y, z_to, c),
            device_id_type=MESH,
        ).wait_recv()

    def across(step, part):
        rows = pl.ds(part * XS, XS)
        return pltpu.make_async_remote_copy(
            src_ref=kv.at[step, rows],
            dst_ref=sib.at[step, rows],
            send_sem=sib_send.at[step, part],
            recv_sem=sib_recv.at[step, part],
            device_id=sibling,
            device_id_type=MESH,
        )

    def last(piece, i, core):
        return pltpu.make_async_remote_copy(
            src_ref=kv.at[HALF - 2, piece],
            dst_ref=far.at[piece],
            send_sem=last_send.at[core, i],
            recv_sem=last_recv.at[piece],
            device_id=device(x, y, z_to, c if core == 0 else 1 - c),
            device_id_type=MESH,
        )

    fetches[3].wait()
    fetches[4].wait()

    lane = lax.broadcasted_iota(jnp.int32, (ROWS, HS), 1)
    own_scores = jnp.zeros((ROWS, HS), jnp.float32)
    group = 2 * xlo + c
    own_key = ok_ref[...].astype(jnp.float32)
    for h in range(GROUP):
        product = qs[group * GROUP + h].astype(jnp.float32) * own_key
        score = jnp.sum(product, axis=1, keepdims=True)
        own_scores = jnp.where(lane == h, score, own_scores)
    own[...] = own_scores

    top[...] = jnp.full(top.shape, -1e30, jnp.float32)
    acc[...] = jnp.zeros(acc.shape, jnp.float32)
    real = lax.broadcasted_iota(jnp.int32, (PIECES, PAD, HS), 1) < KEYS
    ones = jnp.where(real, 1.0, 0.0).astype(jnp.bfloat16).reshape(PIECES * PAD, HS)

    def block_of(held):
        values = held[:, 1].reshape(PIECES * PAD, HS)
        return held[:, 0].reshape(PIECES * PAD, HS), jnp.concatenate([values, ones], axis=1)

    def absorb(i, keys, values):
        scores = nt(qbuf[i].reshape(QB, HS), keys)
        before = top[i]
        best = jnp.max(scores, axis=1, keepdims=True).astype(jnp.bfloat16).astype(jnp.float32)
        now = jnp.maximum(before, jnp.broadcast_to(best, (QB, HS)))
        top[i] = now
        scaled = now * SCALE
        weights = [
            jnp.exp2(scores[:, k : k + HS] * SCALE - scaled).astype(jnp.bfloat16)
            for k in range(0, keys.shape[0], HS)
        ]
        mixed = jnp.dot(
            jnp.concatenate(weights, axis=1), values, preferred_element_type=jnp.float32
        )
        factor = jnp.exp2((before - now) * SCALE)
        acc[i] = acc[i] * jnp.concatenate([factor, factor], axis=1) + mixed

    def compute(*blocks):
        blocks = [block_of(block) for block in blocks]
        keys = jnp.concatenate([block[0] for block in blocks], axis=0)
        values = jnp.concatenate([block[1] for block in blocks], axis=0)
        for i in range(YS):
            absorb(i, keys, values)

    def relay(way):
        return pltpu.make_async_remote_copy(
            src_ref=near.at[PLACE[2]],
            dst_ref=kv.at[0, 2 * PLACE[2] + c],
            send_sem=relay_send.at[way],
            recv_sem=ring_recv.at[0, 2 * PLACE[2] + c],
            device_id=device(x, y, (z_up, z_down)[way], way),
            device_id_type=MESH,
        )

    def near_across():
        return pltpu.make_async_remote_copy(
            src_ref=near.at[pl.ds(0, XS)],
            dst_ref=near.at[pl.ds(XS, XS)],
            send_sem=sib_send.at[HALF - 1, 0],
            recv_sem=sib_recv.at[HALF - 1, 0],
            device_id=sibling,
            device_id_type=MESH,
        )

    def came(dx):
        here(dx).wait_recv()

    came(2)
    for way in (0, 1):
        relay(way).start()
    came(1)
    came(3)
    near_across().start()
    def pass_on(step, send):
        for piece in range(PIECES):
            arrived(step, piece)
            send(step, piece)
            if piece % XS == XS - 1:
                across(step, piece // XS).start()

    def to_next(step, piece):
        forward(step, piece).start()

    def to_both(step, piece):
        @pl.when(c == piece // XS)
        def _():
            for core in (0, 1):
                last(piece, piece % XS, core).start()

    def crossed(step):
        for part in (0, 1):
            across(step, part).wait_recv()

    def turn(step, _):
        pass_on(step, to_next)
        crossed(step - 1)
        compute(sib.at[step - 1], kv.at[step])
        return 0

    pass_on(0, to_next)
    for dy in (1, 2, 3):
        query(dy).wait_recv()

    @pl.when(jnp.logical_not(q_self))
    def _():
        query(0).wait_recv()

    near_across().wait_recv()
    compute(near, kv.at[0])
    lax.fori_loop(1, HALF - 2, turn, 0)
    pass_on(HALF - 2, to_both)
    crossed(HALF - 3)
    compute(sib.at[HALF - 3], kv.at[HALF - 2])
    crossed(HALF - 2)
    compute(sib.at[HALF - 2])
    for piece in range(PIECES):
        pltpu.make_async_remote_copy(
            src_ref=far.at[piece],
            dst_ref=far.at[piece],
            send_sem=last_send.at[0, 0],
            recv_sem=last_recv.at[piece],
            device_id=sibling,
            device_id_type=MESH,
        ).wait_recv()

    def result(dy):
        return pltpu.make_async_remote_copy(
            src_ref=omsg.at[dy],
            dst_ref=orecv.at[(YS - dy) % YS],
            send_sem=o_send.at[dy],
            recv_sem=o_recv.at[(YS - dy) % YS],
            device_id=device(o_x, at_y(dy), z, o_c),
            device_id_type=MESH,
        )

    keys, values = block_of(far)
    for dy in (2, 1, 3, 0):
        absorb(dy, keys, values)
        omsg[dy, 0:GROUP] = acc[dy, :, :HS].astype(jnp.bfloat16).reshape(GROUP, ROWS, HS)
        stats = jnp.zeros((ROWS, HS), jnp.float32)
        for h in range(GROUP):
            rows = slice(h * ROWS, (h + 1) * ROWS)
            total = acc[dy, rows, HS:]
            high = total.astype(jnp.bfloat16).astype(jnp.float32)
            stats = jnp.where(lane == h, top[dy, rows], stats)
            stats = jnp.where(lane == LANES + h, high, stats)
            stats = jnp.where(lane == 2 * LANES + h, total - high, stats)
        omsg[dy, GROUP] = stats.astype(jnp.bfloat16)
        result(dy).start()

    for dx in (1, 2, 3):
        here(dx).wait_send()
    for way in (0, 1):
        relay(way).wait_send()
        for dx in (1, 3, 0):
            first(way, dx).wait_send()
    for dy in (1, 2, 3):
        query(dy).wait_send()

    @pl.when(jnp.logical_not(q_self))
    def _():
        query(0).wait_send()

    def sent(step, _):
        for piece in range(PIECES):
            forward(step, piece).wait_send()
        return 0

    lax.fori_loop(0, HALF - 2, sent, 0)
    for i in range(XS):
        for core in (0, 1):
            last(i, i, core).wait_send()
    near_across().wait_send()

    def across_sent(step, _):
        for part in (0, 1):
            across(step, part).wait_send()
        return 0

    lax.fori_loop(0, HALF - 1, across_sent, 0)

    for dy in range(YS):
        result(dy).wait_recv()
    largest = own[...]
    tops, totals = [], []
    for i in range(YS):
        stats = orecv[i, GROUP].astype(jnp.float32)
        tops.append(stats)
        totals.append(pltpu.roll(stats, HS - LANES, 1) + pltpu.roll(stats, HS - 2 * LANES, 1))
        largest = jnp.maximum(largest, stats)
    own_factor = jnp.exp2((own[...] - largest) * SCALE)
    factors = [jnp.exp2((t - largest) * SCALE) for t in tops]
    total = own_factor
    for factor, part in zip(factors, totals):
        total = total + factor * part
    own_factor = own_factor / total
    factors = [factor / total for factor in factors]
    own_value = ov_ref[...].astype(jnp.float32)
    for h in range(GROUP):
        mixed = own_factor[:, h : h + 1] * own_value
        for i in range(YS):
            mixed = mixed + factors[i][:, h : h + 1] * orecv[i, h].astype(jnp.float32)
        out_ref[:, h * HS : (h + 1) * HS] = mixed.astype(jnp.bfloat16)
    for dy in range(YS):
        result(dy).wait_send()


def local(queries, keys, values, own_keys, own_values):
    vmem = pl.BlockSpec(memory_space=pltpu.VMEM)
    bf16, f32 = jnp.bfloat16, jnp.float32
    dma = pltpu.SemaphoreType.DMA
    return pl.pallas_call(
        kernel,
        out_shape=jax.ShapeDtypeStruct((ROWS, GROUP * HS), bf16),
        in_specs=[pl.BlockSpec(memory_space=pl.ANY)] * 5,
        out_specs=vmem,
        scratch_shapes=[
            pltpu.VMEM((ROWS, KVH * GROUP * HS), bf16),
            pltpu.VMEM((KEYS, KVH * HS), bf16),
            pltpu.VMEM((KEYS, KVH * HS), bf16),
            pltpu.VMEM((ROWS, HS), bf16),
            pltpu.VMEM((ROWS, HS), bf16),
            dma((5,)),
            pltpu.VMEM((PAD, KVH * HS), f32),
            pltpu.VMEM((KVH, 2, PAD, HS), bf16),
            pltpu.VMEM((KVH * GROUP, ROWS, HS), bf16),
            pltpu.VMEM((YS, GROUP, ROWS, HS), bf16),
            pltpu.VMEM((PIECES, 2, PAD, HS), bf16),
            pltpu.VMEM((HALF - 1, PIECES, 2, PAD, HS), bf16),
            pltpu.VMEM((HALF - 1, PIECES, 2, PAD, HS), bf16),
            pltpu.VMEM((PIECES, 2, PAD, HS), bf16),
            pltpu.VMEM((YS, QB, 2 * HS), f32),
            pltpu.VMEM((YS, QB, HS), f32),
            pltpu.VMEM((ROWS, HS), f32),
            pltpu.VMEM((YS, GROUP + 1, ROWS, HS), bf16),
            pltpu.VMEM((YS, GROUP + 1, ROWS, HS), bf16),
            dma((3, XS)),
            dma((2,)),
            dma((HALF - 1, PIECES)),
            dma((HALF - 1, PIECES)),
            dma((2, XS)),
            dma((PIECES,)),
            dma((HALF, 2)),
            dma((HALF, 2)),
            dma((XS,)),
            dma((YS,)),
            dma((YS,)),
            dma((YS,)),
            dma((YS,)),
        ],
        compiler_params=pltpu.CompilerParams(
            collective_id=0, has_side_effects=True, vmem_limit_bytes=60 << 20
        ),
    )(queries, keys, values, own_keys, own_values)


def solution(mesh):
    placed = (
        P("ctx", None),
        P(("ctx", "grp"), None),
        P(("ctx", "grp"), None),
        P("ctx", "grp"),
        P("ctx", "grp"),
    )
    return jax.shard_map(
        local, mesh=mesh, in_specs=placed, out_specs=P("ctx", "grp"), check_vma=False
    )
```

```python
import functools
import math

import jax
import jax.numpy as jnp
from jax import lax
from jax.experimental import pallas as pl
from jax.experimental.pallas import tpu as pltpu
from jax.sharding import PartitionSpec as P

MESH = pl.DeviceIdType.MESH
HS = 128
KVH = 4
GROUP = 12
ROWS = 16
XS, YS, ZS = 4, 4, 16
KEYS = 60
PAD = 64
HALF = ZS // 2
PIECES = 2 * XS
PLACE = (0, 1, 3, 2)
SCALE = math.log2(math.e) / math.sqrt(HS)
QB = GROUP * ROWS
LANES = 16


def device(x, y, z, c):
    return {"ctx": (y * ZS + z) * 2 + x // 2, "grp": lax.rem(x, 2) * 2 + c}


def head_of(x):
    return x // 2 + 2 * (1 - lax.rem(x, 2))


def nt(a, b):
    return lax.dot_general(a, b, (((1,), (1,)), ((), ())), preferred_element_type=jnp.float32)


def kernel(
    q_hbm, k_hbm, v_hbm, ok_hbm, ov_hbm, out_ref,
    q_ref, k_ref, v_ref, ok_ref, ov_ref, in_sem, pad32, kvst, qs, qbuf, near, kv, sib, far, acc, top, own, omsg, orecv,
    first_send, relay_send, ring_send, ring_recv, last_send, last_recv, sib_send, sib_recv,
    near_recv, q_send, q_recv, o_send, o_recv,
):
    fetches = [
        pltpu.make_async_copy(source, to, in_sem.at[i])
        for i, (source, to) in enumerate(
            ((k_hbm, k_ref), (v_hbm, v_ref), (q_hbm, q_ref), (ok_hbm, ok_ref), (ov_hbm, ov_ref))
        )
    ]
    for fetch in fetches:
        fetch.start()
    ctx, grp = lax.axis_index("ctx"), lax.axis_index("grp")
    xhi, z, y = lax.rem(ctx, 2), lax.rem(ctx // 2, ZS), ctx // (2 * ZS)
    xlo, c = grp // 2, lax.rem(grp, 2)
    x = 2 * xhi + xlo
    mine = head_of(x)

    def at_x(dx):
        return lax.rem(x + dx, XS)

    def at_y(dy):
        return lax.rem(y + dy, YS)

    z_up, z_down = lax.rem(z + 1, ZS), lax.rem(z + ZS - 1, ZS)
    z_to = jnp.where(c == 0, z_up, z_down)
    z_from = jnp.where(c == 0, z_down, z_up)
    sibling = device(x, y, z, 1 - c)
    q_self = c == xhi
    q_x = jnp.where(q_self, x, XS - 1 - x)
    o_x, o_c = 2 * c + mine // 2, lax.rem(mine, 2)

    barrier = pltpu.get_barrier_semaphore()

    def greet(to):
        pl.semaphore_signal(barrier, inc=1, device_id=to, device_id_type=MESH)

    for dx in (1, 3, 0):
        for core in (0, 1):
            greet(device(at_x(dx), y, z_from, core))
    greet(device(x, y, z_to, 1 - c))
    for dx in range(1, XS):
        greet(device(at_x(dx), y, z, c))
    greet(sibling)
    for dy in range(1, YS):
        greet(device(q_x, at_y(dy), z, xhi))

    @pl.when(jnp.logical_not(q_self))
    def _():
        greet(device(q_x, y, z, xhi))

    for which, ref in ((0, k_ref), (1, v_ref)):
        fetches[which].wait()
        rows = ref[...].astype(jnp.float32)
        pad32[0:KEYS, :] = rows
        if which == 0:
            pad32[KEYS:PAD, :] = rows[0 : PAD - KEYS, :]
        else:
            pad32[KEYS:PAD, :] = jnp.zeros((PAD - KEYS, KVH * HS), jnp.float32)
        for h in range(KVH):
            kvst[h, which] = pad32[:, h * HS : (h + 1) * HS].astype(jnp.bfloat16)
    expected = 2 * (XS - 1) + 1 + XS - 1 + 1 + YS - 1
    pl.semaphore_wait(barrier, jnp.where(q_self, expected, expected + 1))

    def here(dx):
        to = at_x(dx)
        return pltpu.make_async_remote_copy(
            src_ref=kvst.at[head_of(to)],
            dst_ref=near.at[PLACE[(XS - dx) % XS]],
            send_sem=first_send.at[2, dx],
            recv_sem=near_recv.at[PLACE[(XS - dx) % XS]],
            device_id=device(to, y, z, c),
            device_id_type=MESH,
        )

    def first(way, dx):
        to = at_x(dx)
        return pltpu.make_async_remote_copy(
            src_ref=kvst.at[head_of(to)],
            dst_ref=kv.at[0, 2 * PLACE[(XS - dx) % XS] + c],
            send_sem=first_send.at[way, dx],
            recv_sem=ring_recv.at[0, 2 * PLACE[(XS - dx) % XS] + c],
            device_id=device(to, y, (z_up, z_down)[way], way),
            device_id_type=MESH,
        )

    def query(dy):
        return pltpu.make_async_remote_copy(
            src_ref=qs.at[pl.ds(head_of(q_x) * GROUP, GROUP)],
            dst_ref=qbuf.at[(YS - dy) % YS],
            send_sem=q_send.at[dy],
            recv_sem=q_recv.at[(YS - dy) % YS],
            device_id=device(q_x, at_y(dy), z, xhi),
            device_id_type=MESH,
        )

    here(2).start()
    for way in (0, 1):
        first(way, 0).start()
    for way in (0, 1):
        for dx in (1, 3):
            first(way, dx).start()
    for dx in (1, 3):
        here(dx).start()
    near[0] = kvst[mine]
    fetches[2].wait()
    for h in range(KVH * GROUP):
        qs[h] = q_ref[:, h * HS : (h + 1) * HS]
    for dy in (2, 1, 3):
        query(dy).start()

    @pl.when(jnp.logical_not(q_self))
    def _():
        query(0).start()

    @pl.when(q_self)
    def _():
        qbuf[0] = qs[pl.ds(mine * GROUP, GROUP)]

    def forward(step, piece):
        return pltpu.make_async_remote_copy(
            src_ref=kv.at[step, piece],
            dst_ref=kv.at[step + 1, piece],
            send_sem=ring_send.at[step, piece],
            recv_sem=ring_recv.at[step + 1, piece],
            device_id=device(x, y, z_to, c),
            device_id_type=MESH,
        )

    def arrived(step, piece):
        pltpu.make_async_remote_copy(
            src_ref=kv.at[step, piece],
            dst_ref=kv.at[step, piece],
            send_sem=ring_send.at[step, piece],
            recv_sem=ring_recv.at[step, piece],
            device_id=device(x, y, z_to, c),
            device_id_type=MESH,
        ).wait_recv()

    def across(step, part):
        rows = pl.ds(part * XS, XS)
        return pltpu.make_async_remote_copy(
            src_ref=kv.at[step, rows],
            dst_ref=sib.at[step, rows],
            send_sem=sib_send.at[step, part],
            recv_sem=sib_recv.at[step, part],
            device_id=sibling,
            device_id_type=MESH,
        )

    def last(piece, i, core):
        return pltpu.make_async_remote_copy(
            src_ref=kv.at[HALF - 2, piece],
            dst_ref=far.at[piece],
            send_sem=last_send.at[core, i],
            recv_sem=last_recv.at[piece],
            device_id=device(x, y, z_to, c if core == 0 else 1 - c),
            device_id_type=MESH,
        )

    fetches[3].wait()
    fetches[4].wait()

    lane = lax.broadcasted_iota(jnp.int32, (ROWS, HS), 1)
    own_scores = jnp.zeros((ROWS, HS), jnp.float32)
    group = 2 * xlo + c
    own_key = ok_ref[...].astype(jnp.float32)
    for h in range(GROUP):
        product = qs[group * GROUP + h].astype(jnp.float32) * own_key
        score = jnp.sum(product, axis=1, keepdims=True)
        own_scores = jnp.where(lane == h, score, own_scores)
    own[...] = own_scores

    top[...] = jnp.full(top.shape, -1e30, jnp.float32)
    acc[...] = jnp.zeros(acc.shape, jnp.float32)
    real = lax.broadcasted_iota(jnp.int32, (PIECES, PAD, HS), 1) < KEYS
    ones = jnp.where(real, 1.0, 0.0).astype(jnp.bfloat16).reshape(PIECES * PAD, HS)

    def block_of(held):
        values = held[:, 1].reshape(PIECES * PAD, HS)
        return held[:, 0].reshape(PIECES * PAD, HS), jnp.concatenate([values, ones], axis=1)

    def absorb(i, keys, values):
        scores = nt(qbuf[i].reshape(QB, HS), keys)
        before = top[i]
        best = jnp.max(scores, axis=1, keepdims=True).astype(jnp.bfloat16).astype(jnp.float32)
        now = jnp.maximum(before, jnp.broadcast_to(best, (QB, HS)))
        top[i] = now
        scaled = now * SCALE
        weights = [
            jnp.exp2(scores[:, k : k + HS] * SCALE - scaled).astype(jnp.bfloat16)
            for k in range(0, keys.shape[0], HS)
        ]
        mixed = jnp.dot(
            jnp.concatenate(weights, axis=1), values, preferred_element_type=jnp.float32
        )
        factor = jnp.exp2((before - now) * SCALE)
        acc[i] = acc[i] * jnp.concatenate([factor, factor], axis=1) + mixed

    def compute(parts, *blocks):
        blocks = [block_of(block) for block in blocks]
        keys = jnp.concatenate([block[0] for block in blocks], axis=0)
        values = jnp.concatenate([block[1] for block in blocks], axis=0)
        for i in parts:
            absorb(i, keys, values)

    def relay(way):
        return pltpu.make_async_remote_copy(
            src_ref=near.at[PLACE[2]],
            dst_ref=kv.at[0, 2 * PLACE[2] + c],
            send_sem=relay_send.at[way],
            recv_sem=ring_recv.at[0, 2 * PLACE[2] + c],
            device_id=device(x, y, (z_up, z_down)[way], way),
            device_id_type=MESH,
        )

    def near_across():
        return pltpu.make_async_remote_copy(
            src_ref=near.at[pl.ds(0, XS)],
            dst_ref=near.at[pl.ds(XS, XS)],
            send_sem=sib_send.at[HALF - 1, 0],
            recv_sem=sib_recv.at[HALF - 1, 0],
            device_id=sibling,
            device_id_type=MESH,
        )

    def came(dx):
        here(dx).wait_recv()

    came(2)
    for way in (0, 1):
        relay(way).start()
    came(1)
    came(3)
    near_across().start()
    work_after = {1: (0,), 3: (1,), 5: (2,), 7: (3,)}

    def pass_on(step, send, *blocks):
        for piece in range(PIECES):
            arrived(step, piece)
            send(step, piece)
            if piece % XS == XS - 1:
                across(step, piece // XS).start()
            if blocks and piece in work_after:
                compute(work_after[piece], *blocks)

    def to_next(step, piece):
        forward(step, piece).start()

    def to_both(step, piece):
        @pl.when(c == piece // XS)
        def _():
            for core in (0, 1):
                last(piece, piece % XS, core).start()

    def crossed(step):
        for part in (0, 1):
            across(step, part).wait_recv()

    def turn(step, _):
        crossed(step - 2)
        pass_on(step, to_next, sib.at[step - 2], kv.at[step - 1])
        return 0

    pass_on(0, to_next)
    for dy in (1, 2, 3):
        query(dy).wait_recv()

    @pl.when(jnp.logical_not(q_self))
    def _():
        query(0).wait_recv()

    near_across().wait_recv()
    pass_on(1, to_next, near, kv.at[0])
    lax.fori_loop(2, HALF - 2, turn, 0)
    crossed(HALF - 4)
    pass_on(HALF - 2, to_both, sib.at[HALF - 4], kv.at[HALF - 3])
    crossed(HALF - 3)
    compute(range(YS), sib.at[HALF - 3], kv.at[HALF - 2])
    crossed(HALF - 2)
    compute(range(YS), sib.at[HALF - 2])
    for piece in range(PIECES):
        pltpu.make_async_remote_copy(
            src_ref=far.at[piece],
            dst_ref=far.at[piece],
            send_sem=last_send.at[0, 0],
            recv_sem=last_recv.at[piece],
            device_id=sibling,
            device_id_type=MESH,
        ).wait_recv()

    def result(dy):
        return pltpu.make_async_remote_copy(
            src_ref=omsg.at[dy],
            dst_ref=orecv.at[(YS - dy) % YS],
            send_sem=o_send.at[dy],
            recv_sem=o_recv.at[(YS - dy) % YS],
            device_id=device(o_x, at_y(dy), z, o_c),
            device_id_type=MESH,
        )

    keys, values = block_of(far)
    for dy in (2, 1, 3, 0):
        absorb(dy, keys, values)
        omsg[dy, 0:GROUP] = acc[dy, :, :HS].astype(jnp.bfloat16).reshape(GROUP, ROWS, HS)
        stats = jnp.zeros((ROWS, HS), jnp.float32)
        for h in range(GROUP):
            rows = slice(h * ROWS, (h + 1) * ROWS)
            total = acc[dy, rows, HS:]
            high = total.astype(jnp.bfloat16).astype(jnp.float32)
            stats = jnp.where(lane == h, top[dy, rows], stats)
            stats = jnp.where(lane == LANES + h, high, stats)
            stats = jnp.where(lane == 2 * LANES + h, total - high, stats)
        omsg[dy, GROUP] = stats.astype(jnp.bfloat16)
        result(dy).start()

    for dx in (1, 2, 3):
        here(dx).wait_send()
    for way in (0, 1):
        relay(way).wait_send()
        for dx in (1, 3, 0):
            first(way, dx).wait_send()
    for dy in (1, 2, 3):
        query(dy).wait_send()

    @pl.when(jnp.logical_not(q_self))
    def _():
        query(0).wait_send()

    def sent(step, _):
        for piece in range(PIECES):
            forward(step, piece).wait_send()
        return 0

    lax.fori_loop(0, HALF - 2, sent, 0)
    for i in range(XS):
        for core in (0, 1):
            last(i, i, core).wait_send()
    near_across().wait_send()

    def across_sent(step, _):
        for part in (0, 1):
            across(step, part).wait_send()
        return 0

    lax.fori_loop(0, HALF - 1, across_sent, 0)

    for dy in range(YS):
        result(dy).wait_recv()
    largest = own[...]
    tops, totals = [], []
    for i in range(YS):
        stats = orecv[i, GROUP].astype(jnp.float32)
        tops.append(stats)
        totals.append(pltpu.roll(stats, HS - LANES, 1) + pltpu.roll(stats, HS - 2 * LANES, 1))
        largest = jnp.maximum(largest, stats)
    own_factor = jnp.exp2((own[...] - largest) * SCALE)
    factors = [jnp.exp2((t - largest) * SCALE) for t in tops]
    total = own_factor
    for factor, part in zip(factors, totals):
        total = total + factor * part
    own_factor = own_factor / total
    factors = [factor / total for factor in factors]
    own_value = ov_ref[...].astype(jnp.float32)
    for h in range(GROUP):
        mixed = own_factor[:, h : h + 1] * own_value
        for i in range(YS):
            mixed = mixed + factors[i][:, h : h + 1] * orecv[i, h].astype(jnp.float32)
        out_ref[:, h * HS : (h + 1) * HS] = mixed.astype(jnp.bfloat16)
    for dy in range(YS):
        result(dy).wait_send()


def local(queries, keys, values, own_keys, own_values):
    vmem = pl.BlockSpec(memory_space=pltpu.VMEM)
    bf16, f32 = jnp.bfloat16, jnp.float32
    dma = pltpu.SemaphoreType.DMA
    return pl.pallas_call(
        kernel,
        out_shape=jax.ShapeDtypeStruct((ROWS, GROUP * HS), bf16),
        in_specs=[pl.BlockSpec(memory_space=pl.ANY)] * 5,
        out_specs=vmem,
        scratch_shapes=[
            pltpu.VMEM((ROWS, KVH * GROUP * HS), bf16),
            pltpu.VMEM((KEYS, KVH * HS), bf16),
            pltpu.VMEM((KEYS, KVH * HS), bf16),
            pltpu.VMEM((ROWS, HS), bf16),
            pltpu.VMEM((ROWS, HS), bf16),
            dma((5,)),
            pltpu.VMEM((PAD, KVH * HS), f32),
            pltpu.VMEM((KVH, 2, PAD, HS), bf16),
            pltpu.VMEM((KVH * GROUP, ROWS, HS), bf16),
            pltpu.VMEM((YS, GROUP, ROWS, HS), bf16),
            pltpu.VMEM((PIECES, 2, PAD, HS), bf16),
            pltpu.VMEM((HALF - 1, PIECES, 2, PAD, HS), bf16),
            pltpu.VMEM((HALF - 1, PIECES, 2, PAD, HS), bf16),
            pltpu.VMEM((PIECES, 2, PAD, HS), bf16),
            pltpu.VMEM((YS, QB, 2 * HS), f32),
            pltpu.VMEM((YS, QB, HS), f32),
            pltpu.VMEM((ROWS, HS), f32),
            pltpu.VMEM((YS, GROUP + 1, ROWS, HS), bf16),
            pltpu.VMEM((YS, GROUP + 1, ROWS, HS), bf16),
            dma((3, XS)),
            dma((2,)),
            dma((HALF - 1, PIECES)),
            dma((HALF - 1, PIECES)),
            dma((2, XS)),
            dma((PIECES,)),
            dma((HALF, 2)),
            dma((HALF, 2)),
            dma((XS,)),
            dma((YS,)),
            dma((YS,)),
            dma((YS,)),
            dma((YS,)),
        ],
        compiler_params=pltpu.CompilerParams(
            collective_id=0, has_side_effects=True, vmem_limit_bytes=60 << 20
        ),
    )(queries, keys, values, own_keys, own_values)


def solution(mesh):
    placed = (
        P("ctx", None),
        P(("ctx", "grp"), None),
        P(("ctx", "grp"), None),
        P("ctx", "grp"),
        P("ctx", "grp"),
    )
    return jax.shard_map(
        local, mesh=mesh, in_specs=placed, out_specs=P("ctx", "grp"), check_vma=False
    )
```

```python
import functools
import math

import jax
import jax.numpy as jnp
from jax import lax
from jax.experimental import pallas as pl
from jax.experimental.pallas import tpu as pltpu
from jax.sharding import PartitionSpec as P

MESH = pl.DeviceIdType.MESH
HS = 128
KVH = 4
GROUP = 12
ROWS = 16
XS, YS, ZS = 4, 4, 16
KEYS = 60
PAD = 64
HALF = ZS // 2
PIECES = 2 * XS
PLACE = (0, 1, 3, 2)
SCALE = math.log2(math.e) / math.sqrt(HS)
QB = GROUP * ROWS
LANES = 16


def device(x, y, z, c):
    return {"ctx": (y * ZS + z) * 2 + x // 2, "grp": lax.rem(x, 2) * 2 + c}


def head_of(x):
    return x // 2 + 2 * (1 - lax.rem(x, 2))


def nt(a, b):
    return lax.dot_general(a, b, (((1,), (1,)), ((), ())), preferred_element_type=jnp.float32)


def kernel(
    q_hbm, k_hbm, v_hbm, ok_hbm, ov_hbm, out_ref,
    q_ref, k_ref, v_ref, ok_ref, ov_ref, in_sem, pad32, kvst, qs, qbuf, near, kv, sib, far, acc, top, own, omsg, orecv,
    first_send, relay_send, ring_send, ring_recv, last_send, last_recv, sib_send, sib_recv,
    near_recv, q_send, q_recv, o_send, o_recv,
):
    fetches = [
        pltpu.make_async_copy(source, to, in_sem.at[i])
        for i, (source, to) in enumerate(
            ((k_hbm, k_ref), (v_hbm, v_ref), (q_hbm, q_ref), (ok_hbm, ok_ref), (ov_hbm, ov_ref))
        )
    ]
    for fetch in fetches:
        fetch.start()
    ctx, grp = lax.axis_index("ctx"), lax.axis_index("grp")
    xhi, z, y = lax.rem(ctx, 2), lax.rem(ctx // 2, ZS), ctx // (2 * ZS)
    xlo, c = grp // 2, lax.rem(grp, 2)
    x = 2 * xhi + xlo
    mine = head_of(x)

    def at_x(dx):
        return lax.rem(x + dx, XS)

    def at_y(dy):
        return lax.rem(y + dy, YS)

    z_up, z_down = lax.rem(z + 1, ZS), lax.rem(z + ZS - 1, ZS)
    z_to = jnp.where(c == 0, z_up, z_down)
    z_from = jnp.where(c == 0, z_down, z_up)
    sibling = device(x, y, z, 1 - c)
    q_self = c == xhi
    q_x = jnp.where(q_self, x, XS - 1 - x)
    o_x, o_c = 2 * c + mine // 2, lax.rem(mine, 2)

    barrier = pltpu.get_barrier_semaphore()

    def greet(to):
        pl.semaphore_signal(barrier, inc=1, device_id=to, device_id_type=MESH)

    for dx in (1, 3, 0):
        for core in (0, 1):
            greet(device(at_x(dx), y, z_from, core))
    greet(device(x, y, z_to, 1 - c))
    for dx in range(1, XS):
        greet(device(at_x(dx), y, z, c))
    greet(sibling)
    for dy in range(1, YS):
        greet(device(q_x, at_y(dy), z, xhi))

    @pl.when(jnp.logical_not(q_self))
    def _():
        greet(device(q_x, y, z, xhi))

    for which, ref in ((0, k_ref), (1, v_ref)):
        fetches[which].wait()
        rows = ref[...].astype(jnp.float32)
        pad32[0:KEYS, :] = rows
        if which == 0:
            pad32[KEYS:PAD, :] = rows[0 : PAD - KEYS, :]
        else:
            pad32[KEYS:PAD, :] = jnp.zeros((PAD - KEYS, KVH * HS), jnp.float32)
        for h in range(KVH):
            kvst[h, which] = pad32[:, h * HS : (h + 1) * HS].astype(jnp.bfloat16)
    expected = 2 * (XS - 1) + 1 + XS - 1 + 1 + YS - 1
    pl.semaphore_wait(barrier, jnp.where(q_self, expected, expected + 1))

    def here(dx):
        to = at_x(dx)
        return pltpu.make_async_remote_copy(
            src_ref=kvst.at[head_of(to)],
            dst_ref=near.at[PLACE[(XS - dx) % XS]],
            send_sem=first_send.at[2, dx],
            recv_sem=near_recv.at[PLACE[(XS - dx) % XS]],
            device_id=device(to, y, z, c),
            device_id_type=MESH,
        )

    def first(way, dx):
        to = at_x(dx)
        return pltpu.make_async_remote_copy(
            src_ref=kvst.at[head_of(to)],
            dst_ref=kv.at[0, 2 * PLACE[(XS - dx) % XS] + c],
            send_sem=first_send.at[way, dx],
            recv_sem=ring_recv.at[0, 2 * PLACE[(XS - dx) % XS] + c],
            device_id=device(to, y, (z_up, z_down)[way], way),
            device_id_type=MESH,
        )

    def query(dy):
        return pltpu.make_async_remote_copy(
            src_ref=qs.at[pl.ds(head_of(q_x) * GROUP, GROUP)],
            dst_ref=qbuf.at[(YS - dy) % YS],
            send_sem=q_send.at[dy],
            recv_sem=q_recv.at[(YS - dy) % YS],
            device_id=device(q_x, at_y(dy), z, xhi),
            device_id_type=MESH,
        )

    here(2).start()
    for way in (0, 1):
        first(way, 0).start()
    for way in (0, 1):
        for dx in (1, 3):
            first(way, dx).start()
    for dx in (1, 3):
        here(dx).start()
    near[0] = kvst[mine]
    fetches[2].wait()
    for h in range(KVH * GROUP):
        qs[h] = q_ref[:, h * HS : (h + 1) * HS]
    def forward(step, piece):
        return pltpu.make_async_remote_copy(
            src_ref=kv.at[step, piece],
            dst_ref=kv.at[step + 1, piece],
            send_sem=ring_send.at[step, piece],
            recv_sem=ring_recv.at[step + 1, piece],
            device_id=device(x, y, z_to, c),
            device_id_type=MESH,
        )

    def arrived(step, piece):
        pltpu.make_async_remote_copy(
            src_ref=kv.at[step, piece],
            dst_ref=kv.at[step, piece],
            send_sem=ring_send.at[step, piece],
            recv_sem=ring_recv.at[step, piece],
            device_id=device(x, y, z_to, c),
            device_id_type=MESH,
        ).wait_recv()

    def across(step, part):
        rows = pl.ds(part * XS, XS)
        return pltpu.make_async_remote_copy(
            src_ref=kv.at[step, rows],
            dst_ref=sib.at[step, rows],
            send_sem=sib_send.at[step, part],
            recv_sem=sib_recv.at[step, part],
            device_id=sibling,
            device_id_type=MESH,
        )

    def last(piece, i, core):
        return pltpu.make_async_remote_copy(
            src_ref=kv.at[HALF - 2, piece],
            dst_ref=far.at[piece],
            send_sem=last_send.at[core, i],
            recv_sem=last_recv.at[piece],
            device_id=device(x, y, z_to, c if core == 0 else 1 - c),
            device_id_type=MESH,
        )

    fetches[3].wait()
    fetches[4].wait()

    lane = lax.broadcasted_iota(jnp.int32, (ROWS, HS), 1)
    own_scores = jnp.zeros((ROWS, HS), jnp.float32)
    group = 2 * xlo + c
    own_key = ok_ref[...].astype(jnp.float32)
    for h in range(GROUP):
        product = qs[group * GROUP + h].astype(jnp.float32) * own_key
        score = jnp.sum(product, axis=1, keepdims=True)
        own_scores = jnp.where(lane == h, score, own_scores)
    own[...] = own_scores

    top[...] = jnp.full(top.shape, -1e30, jnp.float32)
    acc[...] = jnp.zeros(acc.shape, jnp.float32)
    real = lax.broadcasted_iota(jnp.int32, (PIECES, PAD, HS), 1) < KEYS
    ones = jnp.where(real, 1.0, 0.0).astype(jnp.bfloat16).reshape(PIECES * PAD, HS)

    def block_of(held):
        values = held[:, 1].reshape(PIECES * PAD, HS)
        return held[:, 0].reshape(PIECES * PAD, HS), jnp.concatenate([values, ones], axis=1)

    def absorb(i, keys, values):
        scores = nt(qbuf[i].reshape(QB, HS), keys)
        before = top[i]
        best = jnp.max(scores, axis=1, keepdims=True).astype(jnp.bfloat16).astype(jnp.float32)
        now = jnp.maximum(before, jnp.broadcast_to(best, (QB, HS)))
        top[i] = now
        scaled = now * SCALE
        weights = [
            jnp.exp2(scores[:, k : k + HS] * SCALE - scaled).astype(jnp.bfloat16)
            for k in range(0, keys.shape[0], HS)
        ]
        mixed = jnp.dot(
            jnp.concatenate(weights, axis=1), values, preferred_element_type=jnp.float32
        )
        factor = jnp.exp2((before - now) * SCALE)
        acc[i] = acc[i] * jnp.concatenate([factor, factor], axis=1) + mixed

    def compute(parts, *blocks):
        blocks = [block_of(block) for block in blocks]
        keys = jnp.concatenate([block[0] for block in blocks], axis=0)
        values = jnp.concatenate([block[1] for block in blocks], axis=0)
        for i in parts:
            absorb(i, keys, values)

    def relay(way):
        return pltpu.make_async_remote_copy(
            src_ref=near.at[PLACE[2]],
            dst_ref=kv.at[0, 2 * PLACE[2] + c],
            send_sem=relay_send.at[way],
            recv_sem=ring_recv.at[0, 2 * PLACE[2] + c],
            device_id=device(x, y, (z_up, z_down)[way], way),
            device_id_type=MESH,
        )

    def near_across():
        return pltpu.make_async_remote_copy(
            src_ref=near.at[pl.ds(0, XS)],
            dst_ref=near.at[pl.ds(XS, XS)],
            send_sem=sib_send.at[HALF - 1, 0],
            recv_sem=sib_recv.at[HALF - 1, 0],
            device_id=sibling,
            device_id_type=MESH,
        )

    def came(dx):
        here(dx).wait_recv()

    came(2)
    for way in (0, 1):
        relay(way).start()
    for dy in (2, 1, 3):
        query(dy).start()

    @pl.when(jnp.logical_not(q_self))
    def _():
        query(0).start()

    @pl.when(q_self)
    def _():
        qbuf[0] = qs[pl.ds(mine * GROUP, GROUP)]

    came(1)
    came(3)
    near_across().start()
    def left(step):
        for piece in range(PIECES):
            forward(step, piece).wait_send()
        for part in (0, 1):
            across(step, part).wait_send()

    work_after = {1: (0,), 3: (1,), 5: (2,), 7: (3,)}

    def pass_on(step, send, *blocks):
        for piece in range(PIECES):
            arrived(step, piece)
            send(step, piece)
            if piece == PIECES - 1:
                for part in (0, 1):
                    across(step, part).start()
            if blocks and piece == PIECES - 1:
                left(step - 1)
            if blocks and piece in work_after:
                compute(work_after[piece], *blocks)

    def to_next(step, piece):
        forward(step, piece).start()

    def to_both(step, piece):
        @pl.when(c == piece // XS)
        def _():
            for core in (0, 1):
                last(piece, piece % XS, core).start()

    def crossed(step):
        for part in (0, 1):
            across(step, part).wait_recv()

    def turn(step, _):
        crossed(step - 2)
        pass_on(step, to_next, sib.at[step - 2], kv.at[step - 1])
        return 0

    pass_on(0, to_next)
    for dy in (1, 2, 3):
        query(dy).wait_recv()

    @pl.when(jnp.logical_not(q_self))
    def _():
        query(0).wait_recv()

    near_across().wait_recv()
    pass_on(1, to_next, near, kv.at[0])
    for dx in (1, 2, 3):
        here(dx).wait_send()
    for way in (0, 1):
        relay(way).wait_send()
        for dx in (1, 3, 0):
            first(way, dx).wait_send()
    for dy in (1, 2, 3):
        query(dy).wait_send()

    @pl.when(jnp.logical_not(q_self))
    def _():
        query(0).wait_send()

    lax.fori_loop(2, HALF - 2, turn, 0)
    crossed(HALF - 4)
    pass_on(HALF - 2, to_both, sib.at[HALF - 4], kv.at[HALF - 3])
    crossed(HALF - 3)
    compute(range(YS), sib.at[HALF - 3], kv.at[HALF - 2])
    crossed(HALF - 2)
    compute(range(YS), sib.at[HALF - 2])
    for piece in range(PIECES):
        pltpu.make_async_remote_copy(
            src_ref=far.at[piece],
            dst_ref=far.at[piece],
            send_sem=last_send.at[0, 0],
            recv_sem=last_recv.at[piece],
            device_id=sibling,
            device_id_type=MESH,
        ).wait_recv()

    def result(dy):
        return pltpu.make_async_remote_copy(
            src_ref=omsg.at[dy],
            dst_ref=orecv.at[(YS - dy) % YS],
            send_sem=o_send.at[dy],
            recv_sem=o_recv.at[(YS - dy) % YS],
            device_id=device(o_x, at_y(dy), z, o_c),
            device_id_type=MESH,
        )

    keys, values = block_of(far)
    for dy in (2, 1, 3, 0):
        absorb(dy, keys, values)
        omsg[dy, 0:GROUP] = acc[dy, :, :HS].astype(jnp.bfloat16).reshape(GROUP, ROWS, HS)
        stats = jnp.zeros((ROWS, HS), jnp.float32)
        for h in range(GROUP):
            rows = slice(h * ROWS, (h + 1) * ROWS)
            total = acc[dy, rows, HS:]
            high = total.astype(jnp.bfloat16).astype(jnp.float32)
            stats = jnp.where(lane == h, top[dy, rows], stats)
            stats = jnp.where(lane == LANES + h, high, stats)
            stats = jnp.where(lane == 2 * LANES + h, total - high, stats)
        omsg[dy, GROUP] = stats.astype(jnp.bfloat16)
        result(dy).start()

    for i in range(XS):
        for core in (0, 1):
            last(i, i, core).wait_send()
    near_across().wait_send()

    for part in (0, 1):
        across(HALF - 2, part).wait_send()

    for dy in range(YS):
        result(dy).wait_recv()
    largest = own[...]
    tops, totals = [], []
    for i in range(YS):
        stats = orecv[i, GROUP].astype(jnp.float32)
        tops.append(stats)
        totals.append(pltpu.roll(stats, HS - LANES, 1) + pltpu.roll(stats, HS - 2 * LANES, 1))
        largest = jnp.maximum(largest, stats)
    own_factor = jnp.exp2((own[...] - largest) * SCALE)
    factors = [jnp.exp2((t - largest) * SCALE) for t in tops]
    total = own_factor
    for factor, part in zip(factors, totals):
        total = total + factor * part
    own_factor = own_factor / total
    factors = [factor / total for factor in factors]
    own_value = ov_ref[...].astype(jnp.float32)
    for h in range(GROUP):
        mixed = own_factor[:, h : h + 1] * own_value
        for i in range(YS):
            mixed = mixed + factors[i][:, h : h + 1] * orecv[i, h].astype(jnp.float32)
        out_ref[:, h * HS : (h + 1) * HS] = mixed.astype(jnp.bfloat16)
    for dy in range(YS):
        result(dy).wait_send()


def local(queries, keys, values, own_keys, own_values):
    vmem = pl.BlockSpec(memory_space=pltpu.VMEM)
    bf16, f32 = jnp.bfloat16, jnp.float32
    dma = pltpu.SemaphoreType.DMA
    return pl.pallas_call(
        kernel,
        out_shape=jax.ShapeDtypeStruct((ROWS, GROUP * HS), bf16),
        in_specs=[pl.BlockSpec(memory_space=pl.ANY)] * 5,
        out_specs=vmem,
        scratch_shapes=[
            pltpu.VMEM((ROWS, KVH * GROUP * HS), bf16),
            pltpu.VMEM((KEYS, KVH * HS), bf16),
            pltpu.VMEM((KEYS, KVH * HS), bf16),
            pltpu.VMEM((ROWS, HS), bf16),
            pltpu.VMEM((ROWS, HS), bf16),
            dma((5,)),
            pltpu.VMEM((PAD, KVH * HS), f32),
            pltpu.VMEM((KVH, 2, PAD, HS), bf16),
            pltpu.VMEM((KVH * GROUP, ROWS, HS), bf16),
            pltpu.VMEM((YS, GROUP, ROWS, HS), bf16),
            pltpu.VMEM((PIECES, 2, PAD, HS), bf16),
            pltpu.VMEM((HALF - 1, PIECES, 2, PAD, HS), bf16),
            pltpu.VMEM((HALF - 1, PIECES, 2, PAD, HS), bf16),
            pltpu.VMEM((PIECES, 2, PAD, HS), bf16),
            pltpu.VMEM((YS, QB, 2 * HS), f32),
            pltpu.VMEM((YS, QB, HS), f32),
            pltpu.VMEM((ROWS, HS), f32),
            pltpu.VMEM((YS, GROUP + 1, ROWS, HS), bf16),
            pltpu.VMEM((YS, GROUP + 1, ROWS, HS), bf16),
            dma((3, XS)),
            dma((2,)),
            dma((HALF - 1, PIECES)),
            dma((HALF - 1, PIECES)),
            dma((2, XS)),
            dma((PIECES,)),
            dma((HALF, 2)),
            dma((HALF, 2)),
            dma((XS,)),
            dma((YS,)),
            dma((YS,)),
            dma((YS,)),
            dma((YS,)),
        ],
        compiler_params=pltpu.CompilerParams(
            collective_id=0, has_side_effects=True, vmem_limit_bytes=60 << 20
        ),
    )(queries, keys, values, own_keys, own_values)


def solution(mesh):
    placed = (
        P("ctx", None),
        P(("ctx", "grp"), None),
        P(("ctx", "grp"), None),
        P("ctx", "grp"),
        P("ctx", "grp"),
    )
    return jax.shard_map(
        local, mesh=mesh, in_specs=placed, out_specs=P("ctx", "grp"), check_vma=False
    )
```
